256 devices in a mesh: ctx: 64 (over z, x, y_lo), head: 4 (over y_hi, core).
Axes of the slice: x: 4, y: 4 (y_hi: 2, y_lo: 2; y = y_hi * 2 + y_lo), z: 8, core: 2. Of those that a mesh axis runs over, the one named last changes fastest.
Arguments:
- queries: bfloat16 [24576, 1024], P('ctx', 'head'), may hold values from -80 to 80
- key_rows: bfloat16 [24576, 128], P(('ctx', 'head')), may hold values from -9 to 9
- value_rows: bfloat16 [24576, 128], P(('ctx', 'head')), may hold values from -6 to 6
- doc_lengths: int32 [64], replicated, may hold values from 1 to 6144, 24576 in all
Outputs:
- attended: bfloat16 [24576, 1024], P('ctx', 'head')
The draws below stay inside these ranges and needn't reach their ends.
Inputs may be any that keep to these rules, and one draw needn't show every extreme that they name: `doc_lengths`: lengths of documents in order; they fill all 24576 positions and the longest has exactly 6144.
All inputs are finite; a program needn't handle non-finite values.
Results may differ from the reference program's by a relative error of at most 0.0045.
Values may be sent and summed in bfloat16 or wider, within the bound.
No kernel may reach another device: no remote copies, remote signals or barrier semaphores. Data moves between devices by JAX's collectives and lax.ppermute only.
A program may use at most 64 MiB of HBM per device.

```python
import math
import jax
import jax.numpy as jnp
import numpy as np
from jax import lax

HEAD_DIM = 128
HEADS = 8
TOK_DEV = 384
TOKENS = 24576
DOC_MOST = 6144
DOCS = 64
N_CTX = 64


def shared_keys(key):
    return jnp.clip(jax.random.normal(key, (TOKENS, HEAD_DIM), jnp.float32), -4.0, 4.0)


def draw_key_rows(key, part):
    base = shared_keys(key)
    return base.astype(jnp.bfloat16)


def draw_queries(key, part):
    key = jax.random.fold_in(key, 7)
    result = 2.0 * jnp.clip(jax.random.normal(key, (TOKENS, HEADS * HEAD_DIM), jnp.float32), -4.0, 4.0)
    return result.astype(jnp.bfloat16)


def steps_of(own_key, shape, pieces, low, high):
    level = 1.0
    for position, blocks in pieces:
        heights = jax.random.uniform(jax.random.fold_in(jax.random.fold_in(own_key, 6), position), (blocks,), jnp.float32, low / len(pieces), high / len(pieces))
        level = level * jnp.repeat(jnp.exp(heights), shape[position] // blocks).reshape((-1,) + (1,) * (len(shape) - 1 - position))
    return level


def length_profile(number_of, total, bound, slope):
    loads = [(1 << 20) // math.isqrt(standing ** slope) + 1 for standing in range(2, number_of + 1)]
    rest, holding = total - bound - (number_of - 1), [1] * (number_of - 1)
    while rest > 0:
        candidates = [i for i in range(number_of - 1) if holding[i] < bound]
        mass, remaining = sum([loads[i] for i in candidates]), rest
        for i in candidates:
            extra = min(bound - holding[i], max(1, remaining * loads[i] // mass), rest)
            holding[i] = holding[i] + extra
            rest = rest - extra
    return np.array([bound] + holding)


def ragged(stream_key, number_of, total, reach, slope):
    if number_of == 2:
        one = jax.random.randint(stream_key, (), max(1, total - reach), min(reach, total - 1) + 1)
        return jnp.stack([one, total - one])
    sizes = jnp.asarray(length_profile(number_of, total, reach, slope), jnp.int32)
    couples = (number_of - 1) // 2
    source_of, sink = sizes[1:1 + 2 * couples:2], sizes[2:2 + 2 * couples:2]
    room = jnp.minimum(source_of - 1, reach - sink)
    passed = jax.random.randint(jax.random.fold_in(stream_key, 1), (couples,), 0, 1 << 20) % (room + 1)
    sizes = sizes.at[1:1 + 2 * couples:2].set(source_of - passed).at[2:2 + 2 * couples:2].set(sink + passed)
    return sizes[jax.random.permutation(jax.random.fold_in(stream_key, 2), number_of)]


def gaussian(own_key, dims, deviation, bound, shards=(), kind=jnp.bfloat16):
    level = steps_of(own_key, dims, shards, -0.22, 0.18) if shards else 1.0
    drawn = jax.random.normal(own_key, dims, jnp.float32) * deviation * level
    return jnp.minimum(jnp.maximum(drawn, -bound), bound).astype(kind)


def setup_inputs(seed: int = 0) -> dict:
    key_list = jax.random.split(jax.random.key(seed), 5)
    return {
        "queries": draw_queries(jax.random.fold_in(key_list[4], 71), 0),
        "key_rows": draw_key_rows(jax.random.fold_in(key_list[4], 71), 0),
        "value_rows": gaussian(key_list[2], (TOKENS, HEAD_DIM), 1.0, 6.0, ((0, 256),)),
        "doc_lengths": ragged(key_list[3], DOCS, TOKENS, DOC_MOST, 2).astype(jnp.int32),
    }


NEG = -1.0e30


def doc_index(positions, doc_ends):
    return jnp.sum((positions[:, None] >= doc_ends[None, :]).astype(jnp.int32), axis=1)


def block_terms(query_heads, q_pos, q_doc, key_block, value_block, k_pos, doc_ends):
    k_doc = doc_index(k_pos, doc_ends)
    allowed = (k_pos[None, :] <= q_pos[:, None]) & (k_doc[None, :] == q_doc[:, None])
    scores = jnp.einsum("qhd,kd->qhk", query_heads.astype(jnp.float32), key_block.astype(jnp.float32)) * (HEAD_DIM ** -0.5)
    scores = jnp.where(allowed[:, None, :], scores, NEG)
    block_max = jnp.max(scores, axis=2)
    weights = jnp.where(allowed[:, None, :], jnp.exp(scores - block_max[:, :, None]), 0.0).astype(jnp.bfloat16)
    weights = lax.optimization_barrier(weights).astype(jnp.float32)
    block_sum = jnp.sum(weights, axis=2)
    partial_value = jnp.einsum("qhk,kd->qhd", weights, value_block.astype(jnp.float32))
    return block_max, block_sum, partial_value


def merge_terms(merged, terms):
    run_max, run_sum, run_out = merged
    block_max, block_sum, partial_value = terms
    newest = jnp.maximum(run_max, block_max)
    old_scale = jnp.exp(run_max - newest)
    new_scale = jnp.exp(block_max - newest)
    return (newest, run_sum * old_scale + block_sum * new_scale,
            run_out * old_scale[:, :, None] + partial_value * new_scale[:, :, None])


def reference(queries, key_rows, value_rows, doc_lengths):
    doc_ends = jnp.cumsum(doc_lengths).astype(jnp.int32)

    def one_block(block_index):
        first_row = (block_index * TOK_DEV).astype(jnp.int32)
        query_heads = lax.dynamic_slice_in_dim(queries, first_row, TOK_DEV, 0).reshape(TOK_DEV, HEADS, HEAD_DIM)
        q_pos = first_row + jnp.arange(TOK_DEV, dtype=jnp.int32)
        q_doc = doc_index(q_pos, doc_ends)
        doc_start = jnp.max(jnp.where(doc_ends <= first_row, doc_ends, 0)).astype(jnp.int32)
        start_block = (doc_start // TOK_DEV).astype(jnp.int32)
        merged = (jnp.full((TOK_DEV, HEADS), NEG, jnp.float32),
                  jnp.zeros((TOK_DEV, HEADS), jnp.float32),
                  jnp.zeros((TOK_DEV, HEADS, HEAD_DIM), jnp.float32))

        def absorb(key_index, merged):
            key_first = (key_index * TOK_DEV).astype(jnp.int32)
            key_block = lax.dynamic_slice_in_dim(key_rows, key_first, TOK_DEV, 0)
            value_block = lax.dynamic_slice_in_dim(value_rows, key_first, TOK_DEV, 0)
            k_pos = key_first + jnp.arange(TOK_DEV, dtype=jnp.int32)
            return merge_terms(merged, block_terms(query_heads, q_pos, q_doc, key_block, value_block, k_pos, doc_ends))

        merged = lax.fori_loop(start_block, block_index + 1, absorb, merged)
        run_max, run_sum, run_out = merged
        result = run_out / run_sum[:, :, None]
        return result.reshape(TOK_DEV, HEADS * HEAD_DIM).astype(jnp.bfloat16)

    attended = lax.map(one_block, jnp.arange(N_CTX, dtype=jnp.int32))
    return attended.reshape(TOKENS, HEADS * HEAD_DIM)
```

```python
import functools
import math

import jax
import jax.numpy as jnp
from jax import lax
from jax.experimental import pallas as pl
from jax.experimental.pallas import tpu as pltpu
from jax.sharding import PartitionSpec as P

NEG = -1e30
FAR = -(1 << 20)

NZ, NX, NY, NC = 8, 4, 4, 2
PAIRS = NZ * NX

BACK_X = (0, 8, 7, 1, 2, 3, 4, 5, 6)
BACK_Y = (0, 8, 4, 0, 0, 0, 4, 4, 4)
TURN_Y = (0, 0, 3, 1, 2, 3, 0, 1, 2)
TILE_CHUNKS = 3


def device_index(pair, y, core):
    z, x = divmod(pair % PAIRS, NX)
    y = y % NY
    return (z * NX * 2 + x * 2 + y % 2) * 4 + (y // 2) * NC + core


def send(array, move):
    pairs = []
    for pair in range(PAIRS):
        for y in range(NY):
            for core in range(NC):
                target = move(pair, y, core)
                if target is not None:
                    pairs.append((device_index(pair, y, core), device_index(*target)))
    return lax.ppermute(array, ("ctx", "head"), sorted(pairs))


def first_axis(by):
    return lambda pair, y, core: (pair + by, y, core) if core == 0 else (pair, y + by, core)


def second_axis(by):
    return lambda pair, y, core: (pair, y + by, core) if core == 0 else (pair + by, y, core)


def later_pair(by, cores=(0, 1)):
    return lambda pair, y, core: (pair + by, y, core) if core in cores else None


def other_core(pair, y, core):
    return (pair, y, 1 - core)


def absorb_tiles(flags, starts, first_tile, kv_ref, q_ref, span_ref, m_ref, l_ref, acc_ref, chunk, row_tile, scale):
    head_dim = q_ref.shape[1]
    rows = q_ref.shape[0]
    keys = TILE_CHUNKS * chunk
    tiles = kv_ref.shape[0] // keys

    def absorb(tile, masked):
        at = pl.ds(pl.multiple_of(tile * keys, keys), keys)
        key_tile = kv_ref[at, :head_dim]
        value_t = kv_ref[at, head_dim:].T
        if masked:
            first = (first_tile + tile) * TILE_CHUNKS
            step = lax.broadcasted_iota(jnp.int32, (chunk, 1), 0)
            k_pos = jnp.concatenate([step + starts[first + i] for i in range(TILE_CHUNKS)], axis=0)
        for j in range(rows // row_tile):
            cols = pl.ds(j * row_tile, row_tile)
            s = lax.dot_general(
                key_tile, q_ref[cols, :], (((1,), (1,)), ((), ())), preferred_element_type=jnp.float32
            )
            if masked:
                allowed = (k_pos >= span_ref[0:1, cols]) & (k_pos <= span_ref[1:2, cols])
                s = jnp.where(allowed, s, NEG)
            m_old = m_ref[0:1, cols]
            m_new = jnp.maximum(m_old, jnp.max(s, axis=0, keepdims=True))
            alpha = jnp.exp2((m_old - m_new) * scale)
            p = jnp.exp2((s - m_new) * scale)
            l_ref[0:1, cols] = l_ref[0:1, cols] * alpha + jnp.sum(p, axis=0, keepdims=True)
            acc_ref[:, cols] = acc_ref[:, cols] * alpha + jnp.dot(
                value_t, p.astype(jnp.bfloat16), preferred_element_type=jnp.float32
            )
            m_ref[0:1, cols] = m_new

    def body(tile, carry):
        flag = flags[first_tile + tile]

        @pl.when(flag == 2)
        def _():
            absorb(tile, False)

        @pl.when(flag == 1)
        def _():
            absorb(tile, True)

        return carry

    lax.fori_loop(0, tiles, body, 0)


def attend_kernel(sets, first_tiles, chunk, row_tile, scale, opening, closing, *refs):
    flags, starts, q_ref, span_ref = refs[:4]
    kv_refs = refs[4 : 4 + sets]
    refs = refs[4 + sets :]
    if not opening:
        m_in, l_in, acc_in = refs[:3]
        refs = refs[3:]
    if closing:
        keep_ref, send_ref, m_ref, l_ref, acc_ref = refs
    else:
        m_ref, l_ref, acc_ref = refs
    if opening:
        m_ref[...] = jnp.full(m_ref.shape, NEG, jnp.float32)
        l_ref[...] = jnp.zeros(l_ref.shape, jnp.float32)
        acc_ref[...] = jnp.zeros(acc_ref.shape, jnp.float32)
    else:
        m_ref[...] = m_in[...]
        l_ref[...] = l_in[...]
        acc_ref[...] = acc_in[...]
    for kv_ref, first_tile in zip(kv_refs, first_tiles):
        absorb_tiles(flags, starts, first_tile, kv_ref, q_ref, span_ref, m_ref, l_ref, acc_ref, chunk, row_tile, scale)
    if closing:
        half = acc_ref.shape[1] // 2
        depth = acc_ref.shape[0]
        for ref, cols in ((keep_ref, slice(0, half)), (send_ref, slice(half, 2 * half))):
            ref[:depth, :] = acc_ref[:, cols]
            ref[depth : depth + 1, :] = m_ref[:, cols]
            ref[depth + 1 : depth + 2, :] = l_ref[:, cols]
            ref[depth + 2 :, :] = jnp.zeros((6, half), jnp.float32)


def attend(flags, starts, q, span, kv_sets, first_tiles, state, closing, chunk, scale, row_tile=768):
    rows, head_dim = q.shape
    smem = pl.BlockSpec(memory_space=pltpu.SMEM)
    vmem = pl.BlockSpec(memory_space=pltpu.VMEM)
    opening = state is None
    state_shapes = [(1, rows), (1, rows), (head_dim, rows)]
    if closing:
        out = [jax.ShapeDtypeStruct((head_dim + 8, rows // 2), jnp.float32)] * 2
        scratch = [pltpu.VMEM(shape, jnp.float32) for shape in state_shapes]
    else:
        out = [jax.ShapeDtypeStruct(shape, jnp.float32) for shape in state_shapes]
        scratch = []
    state = [] if opening else list(state)
    keys = sum(kv.shape[0] for kv in kv_sets)
    return pl.pallas_call(
        functools.partial(attend_kernel, len(kv_sets), first_tiles, chunk, row_tile, scale, opening, closing),
        out_shape=out,
        in_specs=[smem, smem] + [vmem] * (2 + len(kv_sets) + len(state)),
        out_specs=[vmem] * len(out),
        scratch_shapes=scratch,
        compiler_params=pltpu.CompilerParams(vmem_limit_bytes=24 * 1024 * 1024),
        cost_estimate=pl.CostEstimate(
            flops=4 * keys * rows * head_dim, bytes_accessed=4 * rows * head_dim, transcendentals=keys * rows
        ),
    )(flags, starts, q, span, *kv_sets, *state)


def merge_kernel(head_dim, scale, keep_ref, came_ref, out_ref):
    rows = out_ref.shape[0]
    for h in range(out_ref.shape[1] // head_dim):
        cols = slice(h * rows, (h + 1) * rows)
        m_a, m_b = keep_ref[head_dim : head_dim + 1, cols], came_ref[head_dim : head_dim + 1, cols]
        l_a, l_b = keep_ref[head_dim + 1 : head_dim + 2, cols], came_ref[head_dim + 1 : head_dim + 2, cols]
        top = jnp.maximum(m_a, m_b)
        w_a, w_b = jnp.exp2((m_a - top) * scale), jnp.exp2((m_b - top) * scale)
        total = l_a * w_a + l_b * w_b
        w_a, w_b = w_a / total, w_b / total
        result = keep_ref[:head_dim, cols] * w_a + came_ref[:head_dim, cols] * w_b
        out_ref[:, h * head_dim : (h + 1) * head_dim] = result.T.astype(out_ref.dtype)


def merge(keep, came, rows, head_dim, scale):
    vmem = pl.BlockSpec(memory_space=pltpu.VMEM)
    heads = keep.shape[1] // rows
    return pl.pallas_call(
        functools.partial(merge_kernel, head_dim, scale),
        out_shape=jax.ShapeDtypeStruct((rows, heads * head_dim), jnp.bfloat16),
        in_specs=[vmem, vmem],
        out_specs=vmem,
    )(keep, came)


def on_device(queries, key_rows, value_rows, doc_lengths):
    row_count = queries.shape[0]
    chunk, head_dim = key_rows.shape
    heads_here = queries.shape[1] // head_dim
    scale = math.log2(math.e) / math.sqrt(head_dim)
    ctx = lax.axis_index("ctx")
    head = lax.axis_index("head")
    core, y_hi = head % NC, head // NC
    pair, y = ctx // 2, y_hi * 2 + ctx % 2

    own = jnp.concatenate([key_rows, value_rows], axis=1)
    back4 = send(own, later_pair(4))
    other_q = send(queries, other_core)
    x0 = jnp.concatenate([own, back4], axis=0)
    x1, x3, x2 = (send(x0, first_axis(by)) for by in (1, 3, 2))
    xz = send(back4, later_pair(4))
    near = jnp.concatenate(
        [own, xz, x3[chunk:], x1[:chunk], x2[:chunk], x3[:chunk], back4, x1[chunk:], x2[chunk:]], axis=0
    )
    b1, b3, b2 = (send(near, second_axis(by)) for by in (1, 3, 2))
    bz = send(jnp.concatenate([x1[chunk:], x2[chunk:], x3[chunk:]], axis=0), later_pair(4, cores=(1,)))

    doc_ends = jnp.sum(
        jnp.where(
            lax.broadcasted_iota(jnp.int32, (DOCS, DOCS), 0) <= lax.broadcasted_iota(jnp.int32, (DOCS, DOCS), 1),
            doc_lengths[:, None],
            0,
        ),
        axis=0,
    )
    first_row = ctx * row_count
    q_pos = first_row + jnp.arange(row_count, dtype=jnp.int32)
    doc_start = jnp.max(jnp.where(doc_ends[:, None] <= q_pos[None, :], doc_ends[:, None], 0), axis=0)
    span = jnp.tile(jnp.stack([doc_start, q_pos]), (1, 2 * heads_here))

    def start_of(back, turn):
        there = (y - turn) % NY
        return (2 * (pair - back) + there % 2) * row_count + (there // 2) * (NC * chunk) + core * chunk

    back_x, back_y, turn_y = (jnp.array(c, jnp.int32) for c in (BACK_X, BACK_Y, TURN_Y))
    starts = []
    for by in (0, 1, 3, 2):
        starts.append(jnp.where(core == 0, start_of(back_x, by), start_of(back_y + by, turn_y)))
    starts.append(jnp.where(core == 0, FAR, start_of(8, jnp.array([1, 2, 3], jnp.int32))))
    starts = jnp.concatenate(starts)
    ends = starts + (chunk - 1)
    needed = (ends >= doc_start[0]) & (starts <= q_pos[-1])
    full = (starts >= doc_start[-1]) & (ends <= q_pos[0])
    flags = jnp.where(
        jnp.all(full.reshape(-1, TILE_CHUNKS), axis=1), 2, jnp.any(needed.reshape(-1, TILE_CHUNKS), axis=1).astype(jnp.int32)
    )

    q = jnp.concatenate(
        [part[:, h * head_dim : (h + 1) * head_dim] for part in (queries, other_q) for h in range(heads_here)], axis=0
    )
    call = functools.partial(attend, flags, starts, q, span, chunk=chunk, scale=scale)
    state = call([near], (0,), None, False)
    state = call([b1, b3], (3, 6), state, False)
    keep, away = call([b2, bz], (9, 12), state, True)
    came = send(away, other_core)
    return merge(keep, came, row_count, head_dim, scale)


DOCS = 64


def solution(mesh):
    return jax.shard_map(
        on_device,
        mesh=mesh,
        in_specs=(P("ctx", "head"), P(("ctx", "head"), None), P(("ctx", "head"), None), P()),
        out_specs=P("ctx", "head"),
        check_vma=False,
    )
```

```python
import functools
import math

import jax
import jax.numpy as jnp
from jax import lax
from jax.experimental import pallas as pl
from jax.experimental.pallas import tpu as pltpu
from jax.sharding import PartitionSpec as P

NEG = -1e30
FAR = -(1 << 20)

NZ, NX, NY, NC = 8, 4, 4, 2
PAIRS = NZ * NX

WIDE = 8
LAST = 8


def device_index(pair, y, core):
    z, x = divmod(pair, NX)
    y = y % NY
    return (z * NX * 2 + x * 2 + y % 2) * 4 + (y // 2) * NC + core


def send(array, move):
    pairs = []
    for pair in range(PAIRS):
        for y in range(NY):
            for core in range(NC):
                target = move(pair, y, core)
                if target is not None:
                    pairs.append((device_index(pair, y, core), device_index(*target)))
    return lax.ppermute(array, ("ctx", "head"), sorted(pairs))


def later_plane(by):
    return lambda pair, y, core: ((pair + by * NX) % PAIRS, y, core)


def along_x(pair, by):
    return pair - pair % NX + (pair + by) % NX


def first_axis(by):
    return lambda pair, y, core: (along_x(pair, by), y, core) if core == 0 else (pair, y + by, core)


def second_axis(by):
    return lambda pair, y, core: (pair, y + by, core) if core == 0 else (along_x(pair, by), y, core)


def other_core(pair, y, core):
    return (pair, y, 1 - core)


def place(row_count, chunk):
    ctx = lax.axis_index("ctx")
    head = lax.axis_index("head")
    core, y_hi = head % NC, head // NC
    pair, y = ctx // 2, y_hi * 2 + ctx % 2

    def start_of(back, turn):
        there = (y - turn + NY) % NY
        return (2 * (pair - back) + there % 2) * row_count + (there // 2) * (NC * chunk) + core * chunk

    return ctx, core, y, start_of


def near_starts(core, start_of):
    return [jnp.where(core == 0, start_of(i, 0), start_of(i // NY * NX, i % NY)) for i in range(WIDE)]


def far_starts(core, start_of):
    return [start_of(LAST, 0)] + [jnp.where(core == 0, FAR, start_of(LAST, turn)) for turn in (1, 2, 3)]


def side_starts(core, y, start_of, by):
    skip = (y + by) % 2 if by != 2 else 0
    return [
        jnp.where(core == 0, start_of(i + skip, by), start_of(i // NY * NX + by, i % NY)) for i in range(WIDE)
    ]


def last_starts(core, start_of):
    return [jnp.where(core == 0, start_of(LAST, 2), FAR)]


def attend_kernel(names, groups, chunk, scale, opening, *refs):
    lens = refs[0]
    q_refs = refs[1 : 1 + groups]
    kv = dict(zip(names, refs[1 + groups :]))
    refs = refs[1 + groups + len(names) :]
    rows = q_refs[0].shape[0]
    head_dim = kv[names[0]].shape[1] // 2
    heads_here = q_refs[0].shape[1] // head_dim
    row_m, row_l = slice(head_dim, head_dim + 1), slice(head_dim + 1, head_dim + 2)
    state = refs if opening else refs[groups:]
    for group, ref in enumerate(state):
        if opening:
            ref[...] = jnp.zeros(ref.shape, jnp.float32)
            ref[row_m, :] = jnp.full((1, ref.shape[1]), NEG, jnp.float32)
        else:
            ref[...] = refs[group][...]

    ctx, core, y, start_of = place(rows, chunk)
    first_row = ctx * rows
    last_row = first_row + (rows - 1)
    q_pos = first_row + lax.broadcasted_iota(jnp.int32, (1, rows), 1)
    end = jnp.int32(0)
    first_doc = last_doc = jnp.int32(0)
    doc_start = jnp.zeros((1, rows), jnp.int32)
    for i in range(lens.shape[0]):
        end = end + lens[i]
        doc_start = jnp.where(end <= q_pos, end, doc_start)
        first_doc = jnp.where(end <= first_row, end, first_doc)
        last_doc = jnp.where(end <= last_row, end, last_doc)

    def absorb(tile, starts, masked):
        keys = len(starts) * chunk
        key_tile = tile[:, :head_dim]
        value_t = jnp.concatenate([tile[:, head_dim:].T, jnp.ones((16, keys), tile.dtype)], axis=0)
        if masked:
            step = lax.broadcasted_iota(jnp.int32, (chunk, 1), 0)
            past = jnp.concatenate([step + start for start in starts], axis=0) - doc_start
            reach = (q_pos - doc_start).astype(jnp.uint32)
            allowed = past.astype(jnp.uint32) <= reach

        def scores(group, h):
            return lax.dot_general(
                key_tile,
                q_refs[group][:, h * head_dim : (h + 1) * head_dim],
                (((1,), (1,)), ((), ())),
                preferred_element_type=jnp.float32,
            )

        def finish(group, h, p, alpha):
            ref, cols = state[group], slice(h * rows, (h + 1) * rows)
            out = jnp.dot(value_t, p, preferred_element_type=jnp.float32)
            ref[row_l, cols] = ref[row_l, cols] * alpha + out[head_dim : head_dim + 1]
            ref[:head_dim, cols] = ref[:head_dim, cols] * alpha + out[:head_dim]

        heads = [(group, h) for group in range(groups) for h in range(heads_here)]
        ahead = [scores(*heads[0]), scores(*heads[1])]
        waiting = None
        for j, (group, h) in enumerate(heads):
            ref, cols = state[group], slice(h * rows, (h + 1) * rows)
            s = ahead.pop(0)
            if j + 2 < len(heads):
                ahead.append(scores(*heads[j + 2]))
            if masked:
                s = jnp.where(allowed, s, NEG)
            m_old = ref[row_m, cols]
            m_new = jnp.maximum(m_old, jnp.max(s, axis=0, keepdims=True))
            alpha = jnp.exp2((m_old - m_new) * scale)
            p = jnp.exp2((s - m_new) * scale).astype(jnp.bfloat16)
            ref[row_m, cols] = m_new
            if waiting is not None:
                finish(*waiting)
            waiting = (group, h, p, alpha)
        finish(*waiting)

    def absorb_if_needed(load, starts):
        needed = full = None
        for start in starts:
            here = (start + (chunk - 1) >= first_doc) & (start <= last_row)
            whole = (start >= last_doc) & (start + (chunk - 1) <= first_row)
            needed = here if needed is None else needed | here
            full = whole if full is None else full & whole

        @pl.when(full)
        def _():
            absorb(load(), starts, False)

        @pl.when(needed & jnp.logical_not(full))
        def _():
            absorb(load(), starts, True)

    wide = WIDE * chunk
    if "own" in kv:
        absorb_if_needed(lambda: kv["own"][:wide, :], near_starts(core, start_of))
        absorb_if_needed(lambda: kv["own"][wide : wide + NY * chunk, :], far_starts(core, start_of))
    for by in (1, 3, 2):
        if by in kv:
            absorb_if_needed(lambda by=by: kv[by][:wide, :], side_starts(core, y, start_of, by))
    if 2 in kv:
        absorb_if_needed(lambda: kv[2][wide:, :], last_starts(core, start_of))


def attend(lens, qs, kv, states, chunk, head_dim, scale):
    smem = pl.BlockSpec(memory_space=pltpu.SMEM)
    vmem = pl.BlockSpec(memory_space=pltpu.VMEM)
    rows = qs[0].shape[0] * (qs[0].shape[1] // head_dim)
    names, arrays = tuple(kv), list(kv.values())
    keys = sum(array.shape[0] for array in arrays)
    given = list(states or [])
    return pl.pallas_call(
        functools.partial(attend_kernel, names, len(qs), chunk, scale, states is None),
        out_shape=[jax.ShapeDtypeStruct((head_dim + 8, rows), jnp.float32)] * len(qs),
        in_specs=[smem] + [vmem] * (len(qs) + len(arrays) + len(given)),
        out_specs=[vmem] * len(qs),
        compiler_params=pltpu.CompilerParams(vmem_limit_bytes=32 * 1024 * 1024),
        cost_estimate=pl.CostEstimate(
            flops=4 * keys * rows * len(qs) * head_dim,
            bytes_accessed=4 * rows * head_dim,
            transcendentals=keys * rows * len(qs),
        ),
    )(lens, *qs, *arrays, *given)


def join_kernel(k_ref, v_ref, out_ref, sems):
    head_dim = k_ref.shape[1]
    copies = [
        pltpu.make_async_copy(k_ref, out_ref.at[:, :head_dim], sems.at[0]),
        pltpu.make_async_copy(v_ref, out_ref.at[:, head_dim:], sems.at[1]),
    ]
    for copy in copies:
        copy.start()
    for copy in copies:
        copy.wait()


def join(key_rows, value_rows):
    chunk, head_dim = key_rows.shape
    return pl.pallas_call(
        join_kernel,
        out_shape=jax.ShapeDtypeStruct((chunk, 2 * head_dim), key_rows.dtype),
        in_specs=[pl.BlockSpec(memory_space=pltpu.HBM)] * 2,
        out_specs=pl.BlockSpec(memory_space=pltpu.VMEM),
        scratch_shapes=[pltpu.SemaphoreType.DMA((2,))],
        compiler_params=pltpu.CompilerParams(vmem_limit_bytes=4 * 1024 * 1024),
    )(key_rows, value_rows)


def merge_kernel(head_dim, scale, keep_ref, came_ref, out_ref):
    rows = out_ref.shape[0]
    for h in range(out_ref.shape[1] // head_dim):
        cols = slice(h * rows, (h + 1) * rows)
        m_a, m_b = keep_ref[head_dim : head_dim + 1, cols], came_ref[head_dim : head_dim + 1, cols]
        l_a, l_b = keep_ref[head_dim + 1 : head_dim + 2, cols], came_ref[head_dim + 1 : head_dim + 2, cols]
        top = jnp.maximum(m_a, m_b)
        w_a, w_b = jnp.exp2((m_a - top) * scale), jnp.exp2((m_b - top) * scale)
        total = l_a * w_a + l_b * w_b
        w_a, w_b = w_a / total, w_b / total
        result = keep_ref[:head_dim, cols] * w_a + came_ref[:head_dim, cols] * w_b
        out_ref[:, h * head_dim : (h + 1) * head_dim] = result.T.astype(out_ref.dtype)


def merge(keep, came, rows, head_dim, scale):
    vmem = pl.BlockSpec(memory_space=pltpu.VMEM)
    heads = keep.shape[1] // rows
    return pl.pallas_call(
        functools.partial(merge_kernel, head_dim, scale),
        out_shape=jax.ShapeDtypeStruct((rows, heads * head_dim), jnp.bfloat16),
        in_specs=[vmem, vmem],
        out_specs=vmem,
        compiler_params=pltpu.CompilerParams(vmem_limit_bytes=8 * 1024 * 1024),
    )(keep, came)


def on_device(queries, key_rows, value_rows, doc_lengths):
    row_count = queries.shape[0]
    chunk, head_dim = key_rows.shape
    scale = math.log2(math.e) / math.sqrt(head_dim)
    ctx = lax.axis_index("ctx")
    core = lax.axis_index("head") % NC

    own = join(key_rows, value_rows)
    back8 = send(own, later_plane(2))
    back4 = send(own, later_plane(1))
    own, back4, back8, late_q = lax.optimization_barrier((own, back4, back8, queries))
    other_q = send(late_q, other_core)

    def round_x(by):
        return (ctx // 2) % NX + by >= NX

    def first(by):
        wraps = (core == 0) & round_x(by)
        parts = [jnp.where(wraps, back4, own), jnp.where(wraps, back8, back4), back8]
        return send(jnp.concatenate(parts, axis=0), first_axis(by))

    got = {by: first(by) for by in (1, 3, 2)}
    planes = [own, back4, back8]
    held = []
    for i, plane in enumerate(planes):
        held += [plane] + [got[by][i * chunk : (i + 1) * chunk] for by in (1, 2, 3)]
    held = jnp.concatenate(held + [own], axis=0)

    def second(by, chunks):
        begin = jnp.where(core == 0, ctx % 2 if by != 2 else 0, jnp.where(round_x(by), NY, 0))
        return send(lax.dynamic_slice_in_dim(held, begin * chunk, chunks * chunk, 0), second_axis(by))

    b1, b3 = second(1, WIDE), second(3, WIDE)
    call = functools.partial(attend, doc_lengths, chunk=chunk, head_dim=head_dim, scale=scale)
    both = [queries, other_q]
    states = call(both, {"own": held}, None)
    held, *states = lax.optimization_barrier((held, *states))
    b2 = second(2, WIDE + 1)
    states = call(both, {1: b1}, states)
    keep, away = call(both, {3: b3}, states)
    (away,) = call([other_q], {2: b2}, [away])
    came = send(away, other_core)
    (keep,) = call([queries], {2: b2}, [keep])
    return merge(keep, came, row_count, head_dim, scale)


def solution(mesh):
    return jax.shard_map(
        on_device,
        mesh=mesh,
        in_specs=(P("ctx", "head"), P(("ctx", "head"), None), P(("ctx", "head"), None), P()),
        out_specs=P("ctx", "head"),
        check_vma=False,
    )
```

```python
import functools
import math

import jax
import jax.numpy as jnp
from jax import lax
from jax.experimental import pallas as pl
from jax.experimental.pallas import tpu as pltpu
from jax.sharding import PartitionSpec as P

NEG = -1e30
FAR = -(1 << 20)

NZ, NX, NY, NC = 8, 4, 4, 2
PAIRS = NZ * NX

WIDE = 8
LAST = 8

X_FIRST = 1


def device_index(pair, y, core):
    z, x = divmod(pair, NX)
    y = y % NY
    return (z * NX * 2 + x * 2 + y % 2) * 4 + (y // 2) * NC + core


def send(array, move):
    pairs = []
    for pair in range(PAIRS):
        for y in range(NY):
            for core in range(NC):
                target = move(pair, y, core)
                if target is not None:
                    pairs.append((device_index(pair, y, core), device_index(*target)))
    return lax.ppermute(array, ("ctx", "head"), sorted(pairs))


def later_plane(by):
    return lambda pair, y, core: ((pair + by * NX) % PAIRS, y, core)


def along_x(pair, by):
    return pair - pair % NX + (pair + by) % NX


def first_axis(by):
    return lambda pair, y, core: (along_x(pair, by), y, core) if core == X_FIRST else (pair, y + by, core)


def second_axis(by):
    return lambda pair, y, core: (pair, y + by, core) if core == X_FIRST else (along_x(pair, by), y, core)


def other_core(pair, y, core):
    return (pair, y, 1 - core)


def place(row_count, chunk):
    ctx = lax.axis_index("ctx")
    head = lax.axis_index("head")
    core, y_hi = head % NC, head // NC
    pair, y = ctx // 2, y_hi * 2 + ctx % 2

    def start_of(back, turn):
        there = (y - turn + NY) % NY
        return (2 * (pair - back) + there % 2) * row_count + (there // 2) * (NC * chunk) + core * chunk

    return ctx, core, y, start_of


def near_starts(core, start_of):
    return [jnp.where(core == X_FIRST, start_of(i, 0), start_of(i // NY * NX, i % NY)) for i in range(WIDE)]


def far_starts(core, start_of):
    return [start_of(LAST, 0)] + [jnp.where(core == X_FIRST, FAR, start_of(LAST, turn)) for turn in (1, 2, 3)]


def side_starts(core, y, start_of, by):
    skip = (y + by) % 2 if by != 2 else 0
    return [
        jnp.where(core == X_FIRST, start_of(i + skip, by), start_of(i // NY * NX + by, i % NY)) for i in range(WIDE)
    ]


def attend_kernel(names, groups, chunk, scale, opening, *refs):
    docs = refs[0]
    q_refs = refs[1 : 1 + groups]
    kv = dict(zip(names, refs[1 + groups :]))
    refs = refs[1 + groups + len(names) :]
    rows = q_refs[0].shape[0]
    head_dim = kv[names[0]].shape[1] // 2
    heads_here = q_refs[0].shape[1] // head_dim
    row_m, row_l = slice(head_dim, head_dim + 1), slice(head_dim + 1, head_dim + 2)
    state = refs[:groups] if opening else refs[groups:]
    for group, ref in enumerate(state):
        if opening:
            ref[...] = jnp.zeros(ref.shape, jnp.float32)
            ref[row_m, :] = jnp.full((1, ref.shape[1]), NEG, jnp.float32)
        else:
            ref[...] = refs[group][...]

    ctx, core, y, start_of = place(rows, chunk)
    first_row = ctx * rows
    last_row = first_row + (rows - 1)
    q_pos = first_row + lax.broadcasted_iota(jnp.int32, (1, rows), 1)
    if opening:
        end = jnp.int32(0)
        doc_start = jnp.zeros((1, rows), jnp.int32)
        for i in range(docs.shape[0]):
            end = end + docs[i]
            doc_start = jnp.where(end <= q_pos, end, doc_start)
        refs[groups][...] = doc_start
    else:
        doc_start = docs[...]
    first_doc, last_doc = jnp.min(doc_start), jnp.max(doc_start)

    def absorb(tile, starts, masked):
        keys = len(starts) * chunk
        key_tile = tile[:, :head_dim]
        value_t = jnp.concatenate([tile[:, head_dim:].T, jnp.ones((16, keys), tile.dtype)], axis=0)
        if masked:
            step = lax.broadcasted_iota(jnp.int32, (chunk, 1), 0)
            past = jnp.concatenate([step + start for start in starts], axis=0) - doc_start
            reach = (q_pos - doc_start).astype(jnp.uint32)
            allowed = past.astype(jnp.uint32) <= reach

        def scores(group, h):
            return lax.dot_general(
                key_tile,
                q_refs[group][:, h * head_dim : (h + 1) * head_dim],
                (((1,), (1,)), ((), ())),
                preferred_element_type=jnp.float32,
            )

        def finish(group, h, p, alpha):
            ref, cols = state[group], slice(h * rows, (h + 1) * rows)
            out = jnp.dot(value_t, p, preferred_element_type=jnp.float32)
            ref[row_l, cols] = ref[row_l, cols] * alpha + out[head_dim : head_dim + 1]
            ref[:head_dim, cols] = ref[:head_dim, cols] * alpha + out[:head_dim]

        heads = [(group, h) for group in range(groups) for h in range(heads_here)]
        ahead = [scores(*heads[0]), scores(*heads[1])]
        waiting = None
        for j, (group, h) in enumerate(heads):
            ref, cols = state[group], slice(h * rows, (h + 1) * rows)
            s = ahead.pop(0)
            if j + 2 < len(heads):
                ahead.append(scores(*heads[j + 2]))
            if masked:
                s = jnp.where(allowed, s, NEG)
            m_old = ref[row_m, cols]
            m_new = jnp.maximum(m_old, jnp.max(s, axis=0, keepdims=True))
            alpha = jnp.exp2((m_old - m_new) * scale)
            p = jnp.exp2((s - m_new) * scale).astype(jnp.bfloat16)
            ref[row_m, cols] = m_new
            if waiting is not None:
                finish(*waiting)
            waiting = (group, h, p, alpha)
        finish(*waiting)

    def reach_of(starts):
        needed = full = None
        for start in starts:
            here = (start + (chunk - 1) >= first_doc) & (start <= last_row)
            whole = (start >= last_doc) & (start + (chunk - 1) <= first_row)
            needed = here if needed is None else needed | here
            full = whole if full is None else full & whole
        return needed, full

    def absorb_if_needed(ref, begin, starts, halves=False):
        near, far = starts[: len(starts) // 2], starts[len(starts) // 2 :]
        needed, full = reach_of(starts)

        def part(count):
            return ref[begin * chunk : (begin + count) * chunk, :]

        @pl.when(full)
        def _():
            absorb(part(len(starts)), starts, False)

        if halves:
            beyond, _ = reach_of(far)

            @pl.when(needed & jnp.logical_not(beyond))
            def _():
                absorb(part(len(near)), near, True)

            needed = beyond

        @pl.when(needed & jnp.logical_not(full))
        def _():
            absorb(part(len(starts)), starts, True)

    if "own" in kv:
        absorb_if_needed(kv["own"], 0, near_starts(core, start_of), True)
        absorb_if_needed(kv["own"], WIDE, far_starts(core, start_of))
    half = WIDE // 2
    if 2 in kv:
        two = side_starts(core, y, start_of, 2)
        absorb_if_needed(kv[2], 0, two, True)
        absorb_if_needed(kv[2], WIDE, [jnp.where(core == X_FIRST, start_of(LAST, 2), FAR)])
    for by in (1, 3):
        starts = side_starts(core, y, start_of, by)
        if (by, 0) in kv:
            absorb_if_needed(kv[by, 0], 0, starts[:half])
        if (by, 1) in kv:
            absorb_if_needed(kv[by, 1], 0, starts[half:])


def attend(docs, qs, kv, states, chunk, head_dim, scale):
    smem = pl.BlockSpec(memory_space=pltpu.SMEM)
    vmem = pl.BlockSpec(memory_space=pltpu.VMEM)
    rows = qs[0].shape[0] * (qs[0].shape[1] // head_dim)
    names, arrays = tuple(kv), list(kv.values())
    keys = sum(array.shape[0] for array in arrays)
    given = list(states or [])
    out = [jax.ShapeDtypeStruct((head_dim + 8, rows), jnp.float32)] * len(qs)
    if states is None:
        out += [jax.ShapeDtypeStruct((1, qs[0].shape[0]), jnp.int32)]
    return pl.pallas_call(
        functools.partial(attend_kernel, names, len(qs), chunk, scale, states is None),
        out_shape=out,
        in_specs=[smem if states is None else vmem] + [vmem] * (len(qs) + len(arrays) + len(given)),
        out_specs=[vmem] * len(out),
        compiler_params=pltpu.CompilerParams(vmem_limit_bytes=32 * 1024 * 1024),
        cost_estimate=pl.CostEstimate(
            flops=4 * keys * rows * len(qs) * head_dim,
            bytes_accessed=4 * rows * head_dim,
            transcendentals=keys * rows * len(qs),
        ),
    )(docs, *qs, *arrays, *given)


def join_kernel(k_ref, v_ref, out_ref, sems):
    head_dim = k_ref.shape[1]
    copies = [
        pltpu.make_async_copy(k_ref, out_ref.at[:, :head_dim], sems.at[0]),
        pltpu.make_async_copy(v_ref, out_ref.at[:, head_dim:], sems.at[1]),
    ]
    for copy in copies:
        copy.start()
    for copy in copies:
        copy.wait()


def join(key_rows, value_rows):
    chunk, head_dim = key_rows.shape
    return pl.pallas_call(
        join_kernel,
        out_shape=jax.ShapeDtypeStruct((chunk, 2 * head_dim), key_rows.dtype),
        in_specs=[pl.BlockSpec(memory_space=pltpu.HBM)] * 2,
        out_specs=pl.BlockSpec(memory_space=pltpu.VMEM),
        scratch_shapes=[pltpu.SemaphoreType.DMA((2,))],
        compiler_params=pltpu.CompilerParams(vmem_limit_bytes=4 * 1024 * 1024),
    )(key_rows, value_rows)


def merge_kernel(head_dim, scale, keep_ref, came_ref, out_ref):
    rows = out_ref.shape[0]
    for h in range(out_ref.shape[1] // head_dim):
        cols = slice(h * rows, (h + 1) * rows)
        m_a, m_b = keep_ref[head_dim : head_dim + 1, cols], came_ref[head_dim : head_dim + 1, cols]
        l_a, l_b = keep_ref[head_dim + 1 : head_dim + 2, cols], came_ref[head_dim + 1 : head_dim + 2, cols]
        top = jnp.maximum(m_a, m_b)
        w_a, w_b = jnp.exp2((m_a - top) * scale), jnp.exp2((m_b - top) * scale)
        total = l_a * w_a + l_b * w_b
        w_a, w_b = w_a / total, w_b / total
        result = keep_ref[:head_dim, cols] * w_a + came_ref[:head_dim, cols] * w_b
        out_ref[:, h * head_dim : (h + 1) * head_dim] = result.T.astype(out_ref.dtype)


def merge(keep, came, rows, head_dim, scale):
    vmem = pl.BlockSpec(memory_space=pltpu.VMEM)
    heads = keep.shape[1] // rows
    return pl.pallas_call(
        functools.partial(merge_kernel, head_dim, scale),
        out_shape=jax.ShapeDtypeStruct((rows, heads * head_dim), jnp.bfloat16),
        in_specs=[vmem, vmem],
        out_specs=vmem,
        compiler_params=pltpu.CompilerParams(vmem_limit_bytes=8 * 1024 * 1024),
    )(keep, came)


def on_device(queries, key_rows, value_rows, doc_lengths):
    row_count = queries.shape[0]
    chunk, head_dim = key_rows.shape
    scale = math.log2(math.e) / math.sqrt(head_dim)
    ctx = lax.axis_index("ctx")
    core = lax.axis_index("head") % NC

    own = join(key_rows, value_rows)
    back8 = send(own, later_plane(2))
    back4 = send(own, later_plane(1))
    back4, back8, late_q = lax.optimization_barrier((back4, back8, queries))
    other_q = send(late_q, other_core)

    def round_x(by):
        return (ctx // 2) % NX + by >= NX

    def first(by):
        wraps = (core == X_FIRST) & round_x(by)
        parts = [jnp.where(wraps, back4, own), jnp.where(wraps, back8, back4), back8]
        return send(jnp.concatenate(parts, axis=0), first_axis(by))

    got = {by: first(by) for by in (2, 1, 3)}
    planes = [own, back4, back8]
    held = []
    for i, plane in enumerate(planes):
        held += [plane] + [got[by][i * chunk : (i + 1) * chunk] for by in (1, 2, 3)]
    held = jnp.concatenate(held + [own], axis=0)

    def second(by, first, chunks):
        begin = jnp.where(core == X_FIRST, ctx % 2 if by != 2 else 0, jnp.where(round_x(by), NY, 0)) + first
        return send(lax.dynamic_slice_in_dim(held, begin * chunk, chunks * chunk, 0), second_axis(by))

    half = WIDE // 2
    sides = {2: second(2, 0, WIDE + 1)}
    for part in (0, 1):
        for by in (1, 3):
            sides[by, part] = second(by, part * half, half)
    call = functools.partial(attend, chunk=chunk, head_dim=head_dim, scale=scale)
    both = [queries, other_q]
    *states, docs = call(doc_lengths, both, {"own": held}, None)

    def some(*keys):
        return {key: sides[key] for key in keys}

    states = call(docs, both, some(2), states)
    keep, away = call(docs, both, some((1, 0), (3, 0)), states)
    last = some((1, 1), (3, 1))
    (away,) = call(docs, [other_q], last, [away])
    came = send(away, other_core)
    (keep,) = call(docs, [queries], last, [keep])
    return merge(keep, came, row_count, head_dim, scale)


def solution(mesh):
    return jax.shard_map(
        on_device,
        mesh=mesh,
        in_specs=(P("ctx", "head"), P(("ctx", "head"), None), P(("ctx", "head"), None), P()),
        out_specs=P("ctx", "head"),
        check_vma=False,
    )
```

```python
import functools
import math

import jax
import jax.numpy as jnp
from jax import lax
from jax.experimental import pallas as pl
from jax.experimental.pallas import tpu as pltpu
from jax.sharding import PartitionSpec as P

NEG = -1e30
FAR = -(1 << 20)

NZ, NX, NY, NC = 8, 4, 4, 2
PAIRS = NZ * NX

WIDE = 8
LAST = 8
NEAR = 4

X_FIRST = 1


def device_index(pair, y, core):
    z, x = divmod(pair, NX)
    y = y % NY
    return (z * NX * 2 + x * 2 + y % 2) * 4 + (y // 2) * NC + core


def send(array, move):
    pairs = []
    for pair in range(PAIRS):
        for y in range(NY):
            for core in range(NC):
                target = move(pair, y, core)
                if target is not None:
                    pairs.append((device_index(pair, y, core), device_index(*target)))
    return lax.ppermute(array, ("ctx", "head"), sorted(pairs))


def later_plane(by):
    return lambda pair, y, core: ((pair + by * NX) % PAIRS, y, core)


def along_x(pair, by):
    return pair - pair % NX + (pair + by) % NX


def first_axis(by):
    return lambda pair, y, core: (along_x(pair, by), y, core) if core == X_FIRST else (pair, y + by, core)


def second_axis(by):
    return lambda pair, y, core: (pair, y + by, core) if core == X_FIRST else (along_x(pair, by), y, core)


def other_core(pair, y, core):
    return (pair, y, 1 - core)


def place(row_count, chunk):
    ctx = lax.axis_index("ctx")
    head = lax.axis_index("head")
    core, y_hi = head % NC, head // NC
    pair, y = ctx // 2, y_hi * 2 + ctx % 2

    def start_of(back, turn):
        there = (y - turn + NY) % NY
        return (2 * (pair - back) + there % 2) * row_count + (there // 2) * (NC * chunk) + core * chunk

    return ctx, core, y, start_of


def near_starts(core, start_of):
    return [jnp.where(core == X_FIRST, start_of(i, 0), start_of(i // NY * NX, i % NY)) for i in range(WIDE)]


def far_starts(core, start_of):
    return [start_of(LAST, 0)] + [jnp.where(core == X_FIRST, FAR, start_of(LAST, turn)) for turn in (1, 2, 3)]


def side_starts(core, y, start_of, by):
    skip = (y + by) % 2 if by != 2 else 0
    return [
        jnp.where(core == X_FIRST, start_of(i + skip, by), start_of(i // NY * NX + by, i % NY)) for i in range(WIDE)
    ]


def attend_kernel(names, groups, chunk, scale, opening, *refs):
    docs = refs[0]
    q_refs = refs[1 : 1 + groups]
    kv = dict(zip(names, refs[1 + groups :]))
    refs = refs[1 + groups + len(names) :]
    rows = q_refs[0].shape[0]
    head_dim = kv[names[0]].shape[1] // 2
    heads_here = q_refs[0].shape[1] // head_dim
    row_m, row_l = slice(head_dim, head_dim + 1), slice(head_dim + 1, head_dim + 2)
    state = refs[:groups] if opening else refs[groups:]
    for group, ref in enumerate(state):
        if opening:
            ref[...] = jnp.zeros(ref.shape, jnp.float32)
            ref[row_m, :] = jnp.full((1, ref.shape[1]), NEG, jnp.float32)
        else:
            ref[...] = refs[group][...]

    ctx, core, y, start_of = place(rows, chunk)
    first_row = ctx * rows
    last_row = first_row + (rows - 1)
    q_pos = first_row + lax.broadcasted_iota(jnp.int32, (1, rows), 1)
    if opening:
        end = jnp.int32(0)
        doc_start = jnp.zeros((1, rows), jnp.int32)
        for i in range(docs.shape[0]):
            end = end + docs[i]
            doc_start = jnp.where(end <= q_pos, end, doc_start)
        refs[groups][...] = doc_start
    else:
        doc_start = docs[...]
    first_doc, last_doc = jnp.min(doc_start), jnp.max(doc_start)

    def absorb(tiles, masked):
        keys_of, values_of, allowed = [], [], []
        for tile, starts in tiles:
            keys_of.append(tile[:, :head_dim])
            ones = jnp.ones((16, tile.shape[0]), tile.dtype)
            values_of.append(jnp.concatenate([tile[:, head_dim:].T, ones], axis=0))
            if masked:
                step = lax.broadcasted_iota(jnp.int32, (chunk, 1), 0)
                past = jnp.concatenate([step + start for start in starts], axis=0) - doc_start
                allowed.append(past.astype(jnp.uint32) <= (q_pos - doc_start).astype(jnp.uint32))

        def scores(t, group, h):
            return lax.dot_general(
                keys_of[t],
                q_refs[group][:, h * head_dim : (h + 1) * head_dim],
                (((1,), (1,)), ((), ())),
                preferred_element_type=jnp.float32,
            )

        def finish(t, group, h, p, alpha):
            ref, cols = state[group], slice(h * rows, (h + 1) * rows)
            out = jnp.dot(values_of[t], p, preferred_element_type=jnp.float32)
            ref[row_l, cols] = ref[row_l, cols] * alpha + out[head_dim : head_dim + 1]
            ref[:head_dim, cols] = ref[:head_dim, cols] * alpha + out[:head_dim]

        units = [(t, group, h) for t in range(len(tiles)) for group in range(groups) for h in range(heads_here)]
        ahead = [scores(*units[0]), scores(*units[1])]
        waiting = None
        for j, (t, group, h) in enumerate(units):
            ref, cols = state[group], slice(h * rows, (h + 1) * rows)
            s = ahead.pop(0)
            if j + 2 < len(units):
                ahead.append(scores(*units[j + 2]))
            if masked:
                s = jnp.where(allowed[t], s, NEG)
            m_old = ref[row_m, cols]
            m_new = jnp.maximum(m_old, jnp.max(s, axis=0, keepdims=True))
            alpha = jnp.exp2((m_old - m_new) * scale)
            p = jnp.exp2((s - m_new) * scale).astype(jnp.bfloat16)
            ref[row_m, cols] = m_new
            if waiting is not None:
                finish(*waiting)
            waiting = (t, group, h, p, alpha)
        finish(*waiting)

    def reach_of(starts):
        needed, full = [], []
        for start in starts:
            needed.append((start + (chunk - 1) >= first_doc) & (start <= last_row))
            full.append((start >= last_doc) & (start + (chunk - 1) <= first_row))
        return functools.reduce(jnp.logical_or, needed), functools.reduce(jnp.logical_and, full)

    def absorb_needed(parts, may_be_full):
        needed, full = reach_of([start for _, starts in parts for start in starts])
        beyond, _ = reach_of([start for _, starts in parts for start in starts[NEAR:]])

        def tiles(count):
            return [(ref[: len(starts[:count]) * chunk, :], starts[:count]) for ref, starts in parts]

        @pl.when(needed & jnp.logical_not(beyond))
        def _():
            near = tiles(NEAR)
            absorb([(jnp.concatenate([t for t, _ in near], axis=0), [s for _, starts in near for s in starts])], True)

        if may_be_full:

            @pl.when(full)
            def _():
                absorb(tiles(None), False)

            beyond = beyond & jnp.logical_not(full)

        @pl.when(beyond)
        def _():
            absorb(tiles(None), True)

    if "own" in kv:
        absorb_needed([(kv["own"], near_starts(core, start_of) + far_starts(core, start_of))], False)
    if 2 in kv:
        last = jnp.where(core == X_FIRST, start_of(LAST, 2), FAR)
        absorb_needed([(kv[2], side_starts(core, y, start_of, 2) + [last])], False)
    if 1 in kv:
        absorb_needed([(kv[by], side_starts(core, y, start_of, by)) for by in (1, 3)], True)


def attend(docs, qs, kv, states, chunk, head_dim, scale):
    smem = pl.BlockSpec(memory_space=pltpu.SMEM)
    vmem = pl.BlockSpec(memory_space=pltpu.VMEM)
    rows = qs[0].shape[0] * (qs[0].shape[1] // head_dim)
    names, arrays = tuple(kv), list(kv.values())
    keys = sum(array.shape[0] for array in arrays)
    given = list(states or [])
    out = [jax.ShapeDtypeStruct((head_dim + 8, rows), jnp.float32)] * len(qs)
    if states is None:
        out += [jax.ShapeDtypeStruct((1, qs[0].shape[0]), jnp.int32)]
    return pl.pallas_call(
        functools.partial(attend_kernel, names, len(qs), chunk, scale, states is None),
        out_shape=out,
        in_specs=[smem if states is None else vmem] + [vmem] * (len(qs) + len(arrays) + len(given)),
        out_specs=[vmem] * len(out),
        compiler_params=pltpu.CompilerParams(vmem_limit_bytes=32 * 1024 * 1024),
        cost_estimate=pl.CostEstimate(
            flops=4 * keys * rows * len(qs) * head_dim,
            bytes_accessed=4 * rows * head_dim,
            transcendentals=keys * rows * len(qs),
        ),
    )(docs, *qs, *arrays, *given)


def join_kernel(k_ref, v_ref, out_ref, sems):
    head_dim = k_ref.shape[1]
    copies = [
        pltpu.make_async_copy(k_ref, out_ref.at[:, :head_dim], sems.at[0]),
        pltpu.make_async_copy(v_ref, out_ref.at[:, head_dim:], sems.at[1]),
    ]
    for copy in copies:
        copy.start()
    for copy in copies:
        copy.wait()


def join(key_rows, value_rows):
    chunk, head_dim = key_rows.shape
    return pl.pallas_call(
        join_kernel,
        out_shape=jax.ShapeDtypeStruct((chunk, 2 * head_dim), key_rows.dtype),
        in_specs=[pl.BlockSpec(memory_space=pltpu.HBM)] * 2,
        out_specs=pl.BlockSpec(memory_space=pltpu.VMEM),
        scratch_shapes=[pltpu.SemaphoreType.DMA((2,))],
        compiler_params=pltpu.CompilerParams(vmem_limit_bytes=4 * 1024 * 1024),
    )(key_rows, value_rows)


def merge_kernel(head_dim, scale, keep_ref, came_ref, out_ref):
    rows = out_ref.shape[0]
    for h in range(out_ref.shape[1] // head_dim):
        cols = slice(h * rows, (h + 1) * rows)
        m_a, m_b = keep_ref[head_dim : head_dim + 1, cols], came_ref[head_dim : head_dim + 1, cols]
        l_a, l_b = keep_ref[head_dim + 1 : head_dim + 2, cols], came_ref[head_dim + 1 : head_dim + 2, cols]
        top = jnp.maximum(m_a, m_b)
        w_a, w_b = jnp.exp2((m_a - top) * scale), jnp.exp2((m_b - top) * scale)
        total = l_a * w_a + l_b * w_b
        w_a, w_b = w_a / total, w_b / total
        result = keep_ref[:head_dim, cols] * w_a + came_ref[:head_dim, cols] * w_b
        out_ref[:, h * head_dim : (h + 1) * head_dim] = result.T.astype(out_ref.dtype)


def merge(keep, came, rows, head_dim, scale):
    vmem = pl.BlockSpec(memory_space=pltpu.VMEM)
    heads = keep.shape[1] // rows
    return pl.pallas_call(
        functools.partial(merge_kernel, head_dim, scale),
        out_shape=jax.ShapeDtypeStruct((rows, heads * head_dim), jnp.bfloat16),
        in_specs=[vmem, vmem],
        out_specs=vmem,
        compiler_params=pltpu.CompilerParams(vmem_limit_bytes=8 * 1024 * 1024),
    )(keep, came)


def on_device(queries, key_rows, value_rows, doc_lengths):
    row_count = queries.shape[0]
    chunk, head_dim = key_rows.shape
    scale = math.log2(math.e) / math.sqrt(head_dim)
    ctx = lax.axis_index("ctx")
    core = lax.axis_index("head") % NC

    own = join(key_rows, value_rows)
    own, late_q = lax.optimization_barrier((own, queries))
    back8 = send(own, later_plane(2))
    back4 = send(own, later_plane(1))
    other_q = send(late_q, other_core)
    back8, back4, other_q = lax.optimization_barrier((back8, back4, other_q))

    def round_x(by):
        return (ctx // 2) % NX + by >= NX

    def first(by):
        wraps = (core == X_FIRST) & round_x(by)
        parts = [jnp.where(wraps, back4, own), jnp.where(wraps, back8, back4), back8]
        return send(jnp.concatenate(parts, axis=0), first_axis(by))

    got = {by: first(by) for by in (2, 1, 3)}
    planes = [own, back4, back8]
    held = []
    for i, plane in enumerate(planes):
        held += [plane] + [got[by][i * chunk : (i + 1) * chunk] for by in (1, 2, 3)]
    held = jnp.concatenate(held + [own], axis=0)

    def second(by, chunks):
        begin = jnp.where(core == X_FIRST, ctx % 2 if by != 2 else 0, jnp.where(round_x(by), NY, 0))
        return send(lax.dynamic_slice_in_dim(held, begin * chunk, chunks * chunk, 0), second_axis(by))

    sides = {2: second(2, WIDE + 1), 1: second(1, WIDE), 3: second(3, WIDE)}
    last = {by: sides[by] for by in (1, 3)}
    call = functools.partial(attend, chunk=chunk, head_dim=head_dim, scale=scale)
    both = [queries, other_q]
    *states, docs = call(doc_lengths, both, {"own": held}, None)
    keep, away = call(docs, both, {2: sides[2]}, states)
    (away,) = call(docs, [other_q], last, [away])
    came = send(away, other_core)
    (keep,) = call(docs, [queries], last, [keep])
    return merge(keep, came, row_count, head_dim, scale)


def solution(mesh):
    return jax.shard_map(
        on_device,
        mesh=mesh,
        in_specs=(P("ctx", "head"), P(("ctx", "head"), None), P(("ctx", "head"), None), P()),
        out_specs=P("ctx", "head"),
        check_vma=False,
    )
```

```python
import functools
import math

import jax
import jax.numpy as jnp
from jax import lax
from jax.experimental import pallas as pl
from jax.experimental.pallas import tpu as pltpu
from jax.sharding import PartitionSpec as P

NEG = -1e30
FAR = -(1 << 20)

NZ, NX, NY, NC = 8, 4, 4, 2
PAIRS = NZ * NX

WIDE = 8
LAST = 8
NEAR = 4

X_FIRST = 1


def device_index(pair, y, core):
    z, x = divmod(pair, NX)
    y = y % NY
    return (z * NX * 2 + x * 2 + y % 2) * 4 + (y // 2) * NC + core


def send(array, move):
    pairs = []
    for pair in range(PAIRS):
        for y in range(NY):
            for core in range(NC):
                target = move(pair, y, core)
                if target is not None:
                    pairs.append((device_index(pair, y, core), device_index(*target)))
    return lax.ppermute(array, ("ctx", "head"), sorted(pairs))


def later_plane(by):
    return lambda pair, y, core: ((pair + by * NX) % PAIRS, y, core)


def along_x(pair, by):
    return pair - pair % NX + (pair + by) % NX


def first_axis(by):
    return lambda pair, y, core: (along_x(pair, by), y, core) if core == X_FIRST else (pair, y + by, core)


def second_axis(by):
    return lambda pair, y, core: (pair, y + by, core) if core == X_FIRST else (along_x(pair, by), y, core)


def other_core(pair, y, core):
    return (pair, y, 1 - core)


def place(row_count, chunk):
    ctx = lax.axis_index("ctx")
    head = lax.axis_index("head")
    core, y_hi = head % NC, head // NC
    pair, y = ctx // 2, y_hi * 2 + ctx % 2

    def start_of(back, turn):
        there = (y - turn + NY) % NY
        return (2 * (pair - back) + there % 2) * row_count + (there // 2) * (NC * chunk) + core * chunk

    return ctx, core, y, start_of


def near_starts(core, start_of):
    return [jnp.where(core == X_FIRST, start_of(i, 0), start_of(i // NY * NX, i % NY)) for i in range(WIDE)]


def far_starts(core, start_of):
    return [start_of(LAST, 0)] + [jnp.where(core == X_FIRST, FAR, start_of(LAST, turn)) for turn in (1, 2, 3)]


def side_starts(core, y, start_of, by):
    skip = (y + by) % 2 if by != 2 else 0
    return [
        jnp.where(core == X_FIRST, start_of(i + skip, by), start_of(i // NY * NX + by, i % NY)) for i in range(WIDE)
    ]


def attend_kernel(names, groups, chunk, scale, opening, *refs):
    docs = refs[0]
    q_refs = refs[1 : 1 + groups]
    kv = dict(zip(names, refs[1 + groups :]))
    refs = refs[1 + groups + len(names) :]
    rows = q_refs[0].shape[0]
    head_dim = kv[names[0]].shape[1] // 2
    heads_here = q_refs[0].shape[1] // head_dim
    row_m, row_l = slice(head_dim, head_dim + 1), slice(head_dim + 1, head_dim + 2)
    state = refs[:groups] if opening else refs[groups:]
    for group, ref in enumerate(state):
        if opening:
            ref[...] = jnp.zeros(ref.shape, jnp.float32)
            ref[row_m, :] = jnp.full((1, ref.shape[1]), NEG, jnp.float32)
        else:
            ref[...] = refs[group][...]

    ctx, core, y, start_of = place(rows, chunk)
    first_row = ctx * rows
    last_row = first_row + (rows - 1)
    q_pos = first_row + lax.broadcasted_iota(jnp.int32, (1, rows), 1)
    if opening:
        end = jnp.int32(0)
        doc_start = jnp.zeros((1, rows), jnp.int32)
        for i in range(docs.shape[0]):
            end = end + docs[i]
            doc_start = jnp.where(end <= q_pos, end, doc_start)
        refs[groups][...] = doc_start
    else:
        doc_start = docs[...]
    first_doc, last_doc = jnp.min(doc_start), jnp.max(doc_start)

    def absorb(tiles, masked):
        keys_of, values_of, allowed = [], [], []
        for tile, starts in tiles:
            keys_of.append(tile[:, :head_dim])
            ones = jnp.ones((16, tile.shape[0]), tile.dtype)
            values_of.append(jnp.concatenate([tile[:, head_dim:].T, ones], axis=0))
            if masked:
                step = lax.broadcasted_iota(jnp.int32, (chunk, 1), 0)
                past = jnp.concatenate([step + start for start in starts], axis=0) - doc_start
                allowed.append(past.astype(jnp.uint32) <= (q_pos - doc_start).astype(jnp.uint32))

        def scores(t, group, h):
            return lax.dot_general(
                keys_of[t],
                q_refs[group][:, h * head_dim : (h + 1) * head_dim],
                (((1,), (1,)), ((), ())),
                preferred_element_type=jnp.float32,
            )

        def finish(t, group, h, p, alpha):
            ref, cols = state[group], slice(h * rows, (h + 1) * rows)
            out = jnp.dot(values_of[t], p, preferred_element_type=jnp.float32)
            ref[row_l, cols] = ref[row_l, cols] * alpha + out[head_dim : head_dim + 1]
            ref[:head_dim, cols] = ref[:head_dim, cols] * alpha + out[:head_dim]

        units = [(t, group, h) for t in range(len(tiles)) for group in range(groups) for h in range(heads_here)]
        ahead = [scores(*units[0]), scores(*units[1])]
        waiting = None
        for j, (t, group, h) in enumerate(units):
            ref, cols = state[group], slice(h * rows, (h + 1) * rows)
            s = ahead.pop(0)
            if j + 2 < len(units):
                ahead.append(scores(*units[j + 2]))
            if masked:
                s = jnp.where(allowed[t], s, NEG)
            m_old = ref[row_m, cols]
            m_new = jnp.maximum(m_old, jnp.max(s, axis=0, keepdims=True))
            alpha = jnp.exp2((m_old - m_new) * scale)
            p = jnp.exp2((s - m_new) * scale).astype(jnp.bfloat16)
            ref[row_m, cols] = m_new
            if waiting is not None:
                finish(*waiting)
            waiting = (t, group, h, p, alpha)
        finish(*waiting)

    def reach_of(starts):
        needed, full = [], []
        for start in starts:
            needed.append((start + (chunk - 1) >= first_doc) & (start <= last_row))
            full.append((start >= last_doc) & (start + (chunk - 1) <= first_row))
        return functools.reduce(jnp.logical_or, needed), functools.reduce(jnp.logical_and, full)

    def absorb_needed(parts, may_be_full, choose=None):
        needed, full = reach_of([start for _, starts in parts for start in starts])
        beyond, _ = reach_of([start for _, starts in parts for start in starts[NEAR:]])

        def tiles(count):
            return [(ref[: len(starts[:count]) * chunk, :], starts[:count]) for ref, starts in parts]

        if choose is not None:
            picked, places, rest = choose(parts)
            more, _ = reach_of(rest)

            @pl.when(needed & jnp.logical_not(more))
            def _():
                absorb([(picked(), places)], True)

            needed = more

        @pl.when(needed & jnp.logical_not(beyond))
        def _():
            near = tiles(NEAR)
            absorb([(jnp.concatenate([t for t, _ in near], axis=0), [s for _, starts in near for s in starts])], True)

        if may_be_full:

            @pl.when(full)
            def _():
                absorb(tiles(None), False)

            beyond = beyond & jnp.logical_not(full)

        @pl.when(beyond)
        def _():
            absorb(tiles(None), True)

    def nearest(parts):
        (ref, starts), (back_ref, back_starts) = parts
        pick = [jnp.where(core == X_FIRST, a, b) for a, b in zip(back_starts[:2], starts[2:4])]
        left = [jnp.where(core == X_FIRST, b, a) for a, b in zip(back_starts[:2], starts[2:4])]

        def tile():
            other = jnp.where(core == X_FIRST, back_ref[: 2 * chunk, :], ref[2 * chunk : 4 * chunk, :])
            return jnp.concatenate([ref[: 2 * chunk, :], other], axis=0)

        return tile, starts[:2] + pick, starts[4:] + back_starts[2:] + left

    if "own" in kv:
        absorb_needed([(kv["own"], near_starts(core, start_of) + far_starts(core, start_of))], False)
    if 2 in kv:
        last = jnp.where(core == X_FIRST, start_of(LAST, 2), FAR)
        absorb_needed([(kv[2], side_starts(core, y, start_of, 2) + [last])], False)
    if 1 in kv:
        absorb_needed([(kv[by], side_starts(core, y, start_of, by)) for by in (1, 3)], True, nearest)


def attend(docs, qs, kv, states, chunk, head_dim, scale):
    smem = pl.BlockSpec(memory_space=pltpu.SMEM)
    vmem = pl.BlockSpec(memory_space=pltpu.VMEM)
    rows = qs[0].shape[0] * (qs[0].shape[1] // head_dim)
    names, arrays = tuple(kv), list(kv.values())
    keys = sum(array.shape[0] for array in arrays)
    given = list(states or [])
    out = [jax.ShapeDtypeStruct((head_dim + 8, rows), jnp.float32)] * len(qs)
    if states is None:
        out += [jax.ShapeDtypeStruct((1, qs[0].shape[0]), jnp.int32)]
    return pl.pallas_call(
        functools.partial(attend_kernel, names, len(qs), chunk, scale, states is None),
        out_shape=out,
        in_specs=[smem if states is None else vmem] + [vmem] * (len(qs) + len(arrays) + len(given)),
        out_specs=[vmem] * len(out),
        compiler_params=pltpu.CompilerParams(vmem_limit_bytes=32 * 1024 * 1024),
        cost_estimate=pl.CostEstimate(
            flops=4 * keys * rows * len(qs) * head_dim,
            bytes_accessed=4 * rows * head_dim,
            transcendentals=keys * rows * len(qs),
        ),
    )(docs, *qs, *arrays, *given)


def merge_kernel(head_dim, scale, keep_ref, came_ref, out_ref):
    rows = out_ref.shape[0]
    for h in range(out_ref.shape[1] // head_dim):
        cols = slice(h * rows, (h + 1) * rows)
        m_a, m_b = keep_ref[head_dim : head_dim + 1, cols], came_ref[head_dim : head_dim + 1, cols]
        l_a, l_b = keep_ref[head_dim + 1 : head_dim + 2, cols], came_ref[head_dim + 1 : head_dim + 2, cols]
        top = jnp.maximum(m_a, m_b)
        w_a, w_b = jnp.exp2((m_a - top) * scale), jnp.exp2((m_b - top) * scale)
        total = l_a * w_a + l_b * w_b
        w_a, w_b = w_a / total, w_b / total
        result = keep_ref[:head_dim, cols] * w_a + came_ref[:head_dim, cols] * w_b
        out_ref[:, h * head_dim : (h + 1) * head_dim] = result.T.astype(out_ref.dtype)


def merge(keep, came, rows, head_dim, scale):
    vmem = pl.BlockSpec(memory_space=pltpu.VMEM)
    heads = keep.shape[1] // rows
    return pl.pallas_call(
        functools.partial(merge_kernel, head_dim, scale),
        out_shape=jax.ShapeDtypeStruct((rows, heads * head_dim), jnp.bfloat16),
        in_specs=[vmem, vmem],
        out_specs=vmem,
        compiler_params=pltpu.CompilerParams(vmem_limit_bytes=8 * 1024 * 1024),
    )(keep, came)


def on_device(queries, key_rows, value_rows, doc_lengths):
    row_count = queries.shape[0]
    chunk, head_dim = key_rows.shape
    scale = math.log2(math.e) / math.sqrt(head_dim)
    ctx = lax.axis_index("ctx")
    core = lax.axis_index("head") % NC

    own = jnp.concatenate([key_rows, value_rows], axis=1)
    own, late_q = lax.optimization_barrier((own, queries))
    back8 = send(own, later_plane(2))
    back4 = send(own, later_plane(1))
    other_q = send(late_q, other_core)
    back8, back4, other_q = lax.optimization_barrier((back8, back4, other_q))

    def round_x(by):
        return (ctx // 2) % NX + by >= NX

    def first(by):
        wraps = (core == X_FIRST) & round_x(by)
        parts = [jnp.where(wraps, back4, own), jnp.where(wraps, back8, back4), back8]
        return send(jnp.concatenate(parts, axis=0), first_axis(by))

    got = {by: first(by) for by in (2, 1, 3)}
    planes = [own, back4, back8]
    held = []
    for i, plane in enumerate(planes):
        held += [plane] + [got[by][i * chunk : (i + 1) * chunk] for by in (1, 2, 3)]
    held = jnp.concatenate(held + [own], axis=0)

    def second(by, chunks):
        begin = jnp.where(core == X_FIRST, ctx % 2 if by != 2 else 0, jnp.where(round_x(by), NY, 0))
        return send(lax.dynamic_slice_in_dim(held, begin * chunk, chunks * chunk, 0), second_axis(by))

    sides = {2: second(2, WIDE + 1), 1: second(1, WIDE), 3: second(3, WIDE)}
    last = {by: sides[by] for by in (1, 3)}
    call = functools.partial(attend, chunk=chunk, head_dim=head_dim, scale=scale)
    both = [queries, other_q]
    *states, docs = call(doc_lengths, both, {"own": held}, None)
    keep, away = call(docs, both, {2: sides[2]}, states)
    (away,) = call(docs, [other_q], last, [away])
    came = send(away, other_core)
    (keep,) = call(docs, [queries], last, [keep])
    return merge(keep, came, row_count, head_dim, scale)


def solution(mesh):
    return jax.shard_map(
        on_device,
        mesh=mesh,
        in_specs=(P("ctx", "head"), P(("ctx", "head"), None), P(("ctx", "head"), None), P()),
        out_specs=P("ctx", "head"),
        check_vma=False,
    )
```

```python
import functools
import math

import jax
import jax.numpy as jnp
from jax import lax
from jax.experimental import pallas as pl
from jax.experimental.pallas import tpu as pltpu
from jax.sharding import PartitionSpec as P

NEG = -1e30
FAR = -(1 << 20)

NZ, NX, NY, NC = 8, 4, 4, 2
PAIRS = NZ * NX

WIDE = 8
LAST = 8
NEAR = 4

X_FIRST = 1


def device_index(pair, y, core):
    z, x = divmod(pair, NX)
    y = y % NY
    return (z * NX * 2 + x * 2 + y % 2) * 4 + (y // 2) * NC + core


def send(array, move):
    pairs = []
    for pair in range(PAIRS):
        for y in range(NY):
            for core in range(NC):
                target = move(pair, y, core)
                if target is not None:
                    pairs.append((device_index(pair, y, core), device_index(*target)))
    return lax.ppermute(array, ("ctx", "head"), sorted(pairs))


def later_plane(by):
    return lambda pair, y, core: ((pair + by * NX) % PAIRS, y, core)


def along_x(pair, by):
    return pair - pair % NX + (pair + by) % NX


def first_axis(by):
    return lambda pair, y, core: (along_x(pair, by), y, core) if core == X_FIRST else (pair, y + by, core)


def second_axis(by):
    return lambda pair, y, core: (pair, y + by, core) if core == X_FIRST else (along_x(pair, by), y, core)


def other_core(pair, y, core):
    return (pair, y, 1 - core)


def place(row_count, chunk):
    ctx = lax.axis_index("ctx")
    head = lax.axis_index("head")
    core, y_hi = head % NC, head // NC
    pair, y = ctx // 2, y_hi * 2 + ctx % 2

    def start_of(back, turn):
        there = (y - turn + NY) % NY
        return (2 * (pair - back) + there % 2) * row_count + (there // 2) * (NC * chunk) + core * chunk

    return ctx, core, y, start_of


def near_starts(core, start_of):
    return [jnp.where(core == X_FIRST, start_of(i, 0), start_of(i // NY * NX, i % NY)) for i in range(WIDE)]


def far_starts(core, start_of):
    return [start_of(LAST, 0)] + [jnp.where(core == X_FIRST, FAR, start_of(LAST, turn)) for turn in (1, 2, 3)]


def side_starts(core, y, start_of, by):
    skip = (y + by) % 2 if by != 2 else 0
    return [
        jnp.where(core == X_FIRST, start_of(i + skip, by), start_of(i // NY * NX + by, i % NY)) for i in range(WIDE)
    ]


def attend_kernel(names, groups, chunk, scale, opening, *refs):
    docs = refs[0]
    q_refs = refs[1 : 1 + groups]
    kv = dict(zip(names, refs[1 + groups :]))
    refs = refs[1 + groups + len(names) :]
    rows = q_refs[0].shape[0]
    head_dim = kv[names[0]].shape[1] // 2
    heads_here = q_refs[0].shape[1] // head_dim
    row_m, row_l = slice(head_dim, head_dim + 1), slice(head_dim + 1, head_dim + 2)
    state = refs[:groups] if opening else refs[groups:]
    for group, ref in enumerate(state):
        if opening:
            ref[...] = jnp.zeros(ref.shape, jnp.float32)
            ref[row_m, :] = jnp.full((1, ref.shape[1]), NEG, jnp.float32)
        else:
            ref[...] = refs[group][...]

    ctx, core, y, start_of = place(rows, chunk)
    first_row = ctx * rows
    last_row = first_row + (rows - 1)
    q_pos = first_row + lax.broadcasted_iota(jnp.int32, (1, rows), 1)
    if opening:
        end = jnp.int32(0)
        doc_start = jnp.zeros((1, rows), jnp.int32)
        for i in range(docs.shape[0]):
            end = end + docs[i]
            doc_start = jnp.where(end <= q_pos, end, doc_start)
        refs[groups][...] = doc_start
    else:
        doc_start = docs[...]
    first_doc, last_doc = jnp.min(doc_start), jnp.max(doc_start)

    def absorb(tiles, masked):
        keys_of, values_of, allowed = [], [], []
        for tile, starts in tiles:
            keys_of.append(tile[:, :head_dim])
            ones = jnp.ones((16, tile.shape[0]), tile.dtype)
            values_of.append(jnp.concatenate([tile[:, head_dim:].T, ones], axis=0))
            if masked:
                step = lax.broadcasted_iota(jnp.int32, (chunk, 1), 0)
                past = jnp.concatenate([step + start for start in starts], axis=0) - doc_start
                allowed.append(past.astype(jnp.uint32) <= (q_pos - doc_start).astype(jnp.uint32))

        def scores(t, group, h):
            return lax.dot_general(
                keys_of[t],
                q_refs[group][:, h * head_dim : (h + 1) * head_dim],
                (((1,), (1,)), ((), ())),
                preferred_element_type=jnp.float32,
            )

        def finish(t, group, h, p, alpha):
            ref, cols = state[group], slice(h * rows, (h + 1) * rows)
            out = jnp.dot(values_of[t], p, preferred_element_type=jnp.float32)
            ref[row_l, cols] = ref[row_l, cols] * alpha + out[head_dim : head_dim + 1]
            ref[:head_dim, cols] = ref[:head_dim, cols] * alpha + out[:head_dim]

        units = [(t, group, h) for t in range(len(tiles)) for group in range(groups) for h in range(heads_here)]
        ahead = [scores(*units[0]), scores(*units[1])]
        waiting = None
        for j, (t, group, h) in enumerate(units):
            ref, cols = state[group], slice(h * rows, (h + 1) * rows)
            s = ahead.pop(0)
            if j + 2 < len(units):
                ahead.append(scores(*units[j + 2]))
            if masked:
                s = jnp.where(allowed[t], s, NEG)
            m_old = ref[row_m, cols]
            m_new = jnp.maximum(m_old, jnp.max(s, axis=0, keepdims=True))
            alpha = jnp.exp2((m_old - m_new) * scale)
            p = jnp.exp2((s - m_new) * scale).astype(jnp.bfloat16)
            ref[row_m, cols] = m_new
            if waiting is not None:
                finish(*waiting)
            waiting = (t, group, h, p, alpha)
        finish(*waiting)

    def reach_of(starts):
        needed, full = [], []
        for start in starts:
            needed.append((start + (chunk - 1) >= first_doc) & (start <= last_row))
            full.append((start >= last_doc) & (start + (chunk - 1) <= first_row))
        return functools.reduce(jnp.logical_or, needed), functools.reduce(jnp.logical_and, full)

    def absorb_needed(parts, may_be_full, choose=None):
        needed, full = reach_of([start for _, starts in parts for start in starts])
        beyond, _ = reach_of([start for _, starts in parts for start in starts[NEAR:]])

        def tiles(count):
            return [(ref[: len(starts[:count]) * chunk, :], starts[:count]) for ref, starts in parts]

        if choose is not None:
            picked, places, rest = choose(parts)
            more, _ = reach_of(rest)

            @pl.when(needed & jnp.logical_not(more))
            def _():
                absorb([(picked(), places)], True)

            needed = more

        @pl.when(needed & jnp.logical_not(beyond))
        def _():
            near = tiles(NEAR)
            absorb([(jnp.concatenate([t for t, _ in near], axis=0), [s for _, starts in near for s in starts])], True)

        if may_be_full:

            @pl.when(full)
            def _():
                absorb(tiles(None), False)

            beyond = beyond & jnp.logical_not(full)

        @pl.when(beyond)
        def _():
            absorb(tiles(None), True)

    def nearest(parts):
        (ref, starts), (back_ref, back_starts) = parts
        pick = [jnp.where(core == X_FIRST, a, b) for a, b in zip(back_starts[:2], starts[2:4])]
        left = [jnp.where(core == X_FIRST, b, a) for a, b in zip(back_starts[:2], starts[2:4])]

        def tile():
            other = jnp.where(core == X_FIRST, back_ref[: 2 * chunk, :], ref[2 * chunk : 4 * chunk, :])
            return jnp.concatenate([ref[: 2 * chunk, :], other], axis=0)

        return tile, starts[:2] + pick, starts[4:] + back_starts[2:] + left

    if "own" in kv:
        absorb_needed([(kv["own"], near_starts(core, start_of) + far_starts(core, start_of))], False)
    if 2 in kv:
        last = jnp.where(core == X_FIRST, start_of(LAST, 2), FAR)
        absorb_needed([(kv[2], side_starts(core, y, start_of, 2) + [last])], False)
    if 1 in kv:
        absorb_needed([(kv[by], side_starts(core, y, start_of, by)) for by in (1, 3)], True, nearest)


def attend(docs, qs, kv, states, chunk, head_dim, scale):
    smem = pl.BlockSpec(memory_space=pltpu.SMEM)
    vmem = pl.BlockSpec(memory_space=pltpu.VMEM)
    rows = qs[0].shape[0] * (qs[0].shape[1] // head_dim)
    names, arrays = tuple(kv), list(kv.values())
    keys = sum(array.shape[0] for array in arrays)
    given = list(states or [])
    out = [jax.ShapeDtypeStruct((head_dim + 8, rows), jnp.float32)] * len(qs)
    if states is None:
        out += [jax.ShapeDtypeStruct((1, qs[0].shape[0]), jnp.int32)]
    return pl.pallas_call(
        functools.partial(attend_kernel, names, len(qs), chunk, scale, states is None),
        out_shape=out,
        in_specs=[smem if states is None else vmem] + [vmem] * (len(qs) + len(arrays) + len(given)),
        out_specs=[vmem] * len(out),
        compiler_params=pltpu.CompilerParams(vmem_limit_bytes=32 * 1024 * 1024),
        cost_estimate=pl.CostEstimate(
            flops=4 * keys * rows * len(qs) * head_dim,
            bytes_accessed=4 * rows * head_dim,
            transcendentals=keys * rows * len(qs),
        ),
    )(docs, *qs, *arrays, *given)


def merge_kernel(head_dim, scale, keep_ref, came_ref, out_ref):
    rows = out_ref.shape[0]
    for h in range(out_ref.shape[1] // head_dim):
        cols = slice(h * rows, (h + 1) * rows)
        m_a, m_b = keep_ref[head_dim : head_dim + 1, cols], came_ref[head_dim : head_dim + 1, cols]
        l_a, l_b = keep_ref[head_dim + 1 : head_dim + 2, cols], came_ref[head_dim + 1 : head_dim + 2, cols]
        top = jnp.maximum(m_a, m_b)
        w_a, w_b = jnp.exp2((m_a - top) * scale), jnp.exp2((m_b - top) * scale)
        total = l_a * w_a + l_b * w_b
        w_a, w_b = w_a / total, w_b / total
        result = keep_ref[:head_dim, cols] * w_a + came_ref[:head_dim, cols] * w_b
        out_ref[:, h * head_dim : (h + 1) * head_dim] = result.T.astype(out_ref.dtype)


def merge(keep, came, rows, head_dim, scale):
    vmem = pl.BlockSpec(memory_space=pltpu.VMEM)
    heads = keep.shape[1] // rows
    return pl.pallas_call(
        functools.partial(merge_kernel, head_dim, scale),
        out_shape=jax.ShapeDtypeStruct((rows, heads * head_dim), jnp.bfloat16),
        in_specs=[vmem, vmem],
        out_specs=vmem,
        compiler_params=pltpu.CompilerParams(vmem_limit_bytes=8 * 1024 * 1024),
    )(keep, came)


def on_device(queries, key_rows, value_rows, doc_lengths):
    row_count = queries.shape[0]
    chunk, head_dim = key_rows.shape
    scale = math.log2(math.e) / math.sqrt(head_dim)
    ctx = lax.axis_index("ctx")
    core = lax.axis_index("head") % NC

    own = jnp.concatenate([key_rows, value_rows], axis=1)
    own = lax.optimization_barrier(own)
    back8 = send(own, later_plane(2))
    back4 = send(own, later_plane(1))
    back8, back4, late_q = lax.optimization_barrier((back8, back4, queries))
    other_q = send(late_q, other_core)

    def round_x(by):
        return (ctx // 2) % NX + by >= NX

    def first(by):
        wraps = (core == X_FIRST) & round_x(by)
        parts = [jnp.where(wraps, back4, own), jnp.where(wraps, back8, back4), back8]
        return send(jnp.concatenate(parts, axis=0), first_axis(by))

    got = {by: first(by) for by in (2, 1, 3)}
    planes = [own, back4, back8]
    held = []
    for i, plane in enumerate(planes):
        held += [plane] + [got[by][i * chunk : (i + 1) * chunk] for by in (1, 2, 3)]
    held = jnp.concatenate(held + [own], axis=0)

    def second(by, chunks):
        begin = jnp.where(core == X_FIRST, ctx % 2 if by != 2 else 0, jnp.where(round_x(by), NY, 0))
        return send(lax.dynamic_slice_in_dim(held, begin * chunk, chunks * chunk, 0), second_axis(by))

    sides = {2: second(2, WIDE + 1), 1: second(1, WIDE), 3: second(3, WIDE)}
    last = {by: sides[by] for by in (1, 3)}
    call = functools.partial(attend, chunk=chunk, head_dim=head_dim, scale=scale)
    both = [queries, other_q]
    *states, docs = call(doc_lengths, both, {"own": held}, None)
    keep, away = call(docs, both, {2: sides[2]}, states)
    (away,) = call(docs, [other_q], last, [away])
    came = send(away, other_core)
    (keep,) = call(docs, [queries], last, [keep])
    return merge(keep, came, row_count, head_dim, scale)


def solution(mesh):
    return jax.shard_map(
        on_device,
        mesh=mesh,
        in_specs=(P("ctx", "head"), P(("ctx", "head"), None), P(("ctx", "head"), None), P()),
        out_specs=P("ctx", "head"),
        check_vma=False,
    )
```

```python
import functools
import math

import jax
import jax.numpy as jnp
from jax import lax
from jax.experimental import pallas as pl
from jax.experimental.pallas import tpu as pltpu
from jax.sharding import PartitionSpec as P

NEG = -1e30
FAR = -(1 << 20)

NZ, NX, NY, NC = 8, 4, 4, 2
PAIRS = NZ * NX

WIDE = 8
LAST = 8
NEAR = 4

X_FIRST = 1


def device_index(pair, y, core):
    z, x = divmod(pair, NX)
    y = y % NY
    return (z * NX * 2 + x * 2 + y % 2) * 4 + (y // 2) * NC + core


def send(array, move):
    pairs = []
    for pair in range(PAIRS):
        for y in range(NY):
            for core in range(NC):
                target = move(pair, y, core)
                if target is not None:
                    pairs.append((device_index(pair, y, core), device_index(*target)))
    return lax.ppermute(array, ("ctx", "head"), sorted(pairs))


def later_plane(by):
    return lambda pair, y, core: ((pair + by * NX) % PAIRS, y, core)


def along_x(pair, by):
    return pair - pair % NX + (pair + by) % NX


def first_axis(by):
    return lambda pair, y, core: (along_x(pair, by), y, core) if core == X_FIRST else (pair, y + by, core)


def second_axis(by):
    return lambda pair, y, core: (pair, y + by, core) if core == X_FIRST else (along_x(pair, by), y, core)


def other_core(pair, y, core):
    return (pair, y, 1 - core)


def place(row_count, chunk):
    ctx = lax.axis_index("ctx")
    head = lax.axis_index("head")
    core, y_hi = head % NC, head // NC
    pair, y = ctx // 2, y_hi * 2 + ctx % 2

    def start_of(back, turn):
        there = (y - turn + NY) % NY
        return (2 * (pair - back) + there % 2) * row_count + (there // 2) * (NC * chunk) + core * chunk

    return ctx, core, y, start_of


def near_starts(core, start_of):
    return [jnp.where(core == X_FIRST, start_of(i, 0), start_of(i // NY * NX, i % NY)) for i in range(WIDE)]


def far_starts(core, start_of):
    return [start_of(LAST, 0)] + [jnp.where(core == X_FIRST, FAR, start_of(LAST, turn)) for turn in (1, 2, 3)]


def side_starts(core, y, start_of, by):
    skip = (y + by) % 2 if by != 2 else 0
    return [
        jnp.where(core == X_FIRST, start_of(i + skip, by), start_of(i // NY * NX + by, i % NY)) for i in range(WIDE)
    ]


def attend_kernel(names, groups, chunk, scale, opening, *refs):
    docs = refs[0]
    q_refs = refs[1 : 1 + groups]
    kv = dict(zip(names, refs[1 + groups :]))
    refs = refs[1 + groups + len(names) :]
    rows = q_refs[0].shape[0]
    head_dim = kv[names[0]].shape[1] // 2
    heads_here = q_refs[0].shape[1] // head_dim
    row_m, row_l = slice(head_dim, head_dim + 1), slice(head_dim + 1, head_dim + 2)
    state = refs[:groups] if opening else refs[groups:]
    for group, ref in enumerate(state):
        if opening:
            ref[...] = jnp.zeros(ref.shape, jnp.float32)
            ref[row_m, :] = jnp.full((1, ref.shape[1]), NEG, jnp.float32)
        else:
            ref[...] = refs[group][...]

    ctx, core, y, start_of = place(rows, chunk)
    first_row = ctx * rows
    last_row = first_row + (rows - 1)
    q_pos = first_row + lax.broadcasted_iota(jnp.int32, (1, rows), 1)
    if opening:
        end = jnp.int32(0)
        doc_start = jnp.zeros((1, rows), jnp.int32)
        for i in range(docs.shape[0]):
            end = end + docs[i]
            doc_start = jnp.where(end <= q_pos, end, doc_start)
        refs[groups][...] = doc_start
    else:
        doc_start = docs[...]
    first_doc, last_doc = jnp.min(doc_start), jnp.max(doc_start)

    def absorb(tiles, masked):
        keys_of, values_of, allowed = [], [], []
        for tile, starts in tiles:
            keys_of.append(tile[:, :head_dim])
            ones = jnp.ones((16, tile.shape[0]), tile.dtype)
            values_of.append(jnp.concatenate([tile[:, head_dim:].T, ones], axis=0))
            if masked:
                step = lax.broadcasted_iota(jnp.int32, (chunk, 1), 0)
                past = jnp.concatenate([step + start for start in starts], axis=0) - doc_start
                allowed.append(past.astype(jnp.uint32) <= (q_pos - doc_start).astype(jnp.uint32))

        def scores(t, group, h):
            return lax.dot_general(
                keys_of[t],
                q_refs[group][:, h * head_dim : (h + 1) * head_dim],
                (((1,), (1,)), ((), ())),
                preferred_element_type=jnp.float32,
            )

        def finish(t, group, h, p, alpha):
            ref, cols = state[group], slice(h * rows, (h + 1) * rows)
            out = jnp.dot(values_of[t], p, preferred_element_type=jnp.float32)
            ref[row_l, cols] = ref[row_l, cols] * alpha + out[head_dim : head_dim + 1]
            ref[:head_dim, cols] = ref[:head_dim, cols] * alpha + out[:head_dim]

        units = [(t, group, h) for t in range(len(tiles)) for group in range(groups) for h in range(heads_here)]
        ahead = [scores(*units[0]), scores(*units[1])]
        waiting = None
        for j, (t, group, h) in enumerate(units):
            ref, cols = state[group], slice(h * rows, (h + 1) * rows)
            s = ahead.pop(0)
            if j + 2 < len(units):
                ahead.append(scores(*units[j + 2]))
            if masked:
                s = jnp.where(allowed[t], s, NEG)
            m_old = ref[row_m, cols]
            m_new = jnp.maximum(m_old, jnp.max(s, axis=0, keepdims=True))
            alpha = jnp.exp2((m_old - m_new) * scale)
            p = jnp.exp2((s - m_new) * scale).astype(jnp.bfloat16)
            ref[row_m, cols] = m_new
            if waiting is not None:
                finish(*waiting)
            waiting = (t, group, h, p, alpha)
        finish(*waiting)

    def reach_of(starts):
        needed, full = [], []
        for start in starts:
            needed.append((start + (chunk - 1) >= first_doc) & (start <= last_row))
            full.append((start >= last_doc) & (start + (chunk - 1) <= first_row))
        return functools.reduce(jnp.logical_or, needed), functools.reduce(jnp.logical_and, full)

    def absorb_needed(parts, may_be_full, choose=None):
        needed, full = reach_of([start for _, starts in parts for start in starts])
        beyond, _ = reach_of([start for _, starts in parts for start in starts[NEAR:]])

        def tiles(count):
            return [(ref[: len(starts[:count]) * chunk, :], starts[:count]) for ref, starts in parts]

        if choose is not None:
            picked, places, rest = choose(parts)
            more, _ = reach_of(rest)

            @pl.when(needed & jnp.logical_not(more))
            def _():
                absorb([(picked(), places)], True)

            needed = more

        @pl.when(needed & jnp.logical_not(beyond))
        def _():
            near = tiles(NEAR)
            absorb([(jnp.concatenate([t for t, _ in near], axis=0), [s for _, starts in near for s in starts])], True)

        if may_be_full:

            @pl.when(full)
            def _():
                absorb(tiles(None), False)

            beyond = beyond & jnp.logical_not(full)

        @pl.when(beyond)
        def _():
            absorb(tiles(None), True)

    def nearest(parts):
        (ref, starts), (back_ref, back_starts) = parts
        pick = [jnp.where(core == X_FIRST, a, b) for a, b in zip(back_starts[:2], starts[2:4])]
        left = [jnp.where(core == X_FIRST, b, a) for a, b in zip(back_starts[:2], starts[2:4])]

        def tile():
            other = jnp.where(core == X_FIRST, back_ref[: 2 * chunk, :], ref[2 * chunk : 4 * chunk, :])
            return jnp.concatenate([ref[: 2 * chunk, :], other], axis=0)

        return tile, starts[:2] + pick, starts[4:] + back_starts[2:] + left

    if "own" in kv:
        absorb_needed([(kv["own"], near_starts(core, start_of) + far_starts(core, start_of))], False)
    if 2 in kv:
        last = jnp.where(core == X_FIRST, start_of(LAST, 2), FAR)
        absorb_needed([(kv[2], side_starts(core, y, start_of, 2) + [last])], False)
    if 1 in kv:
        absorb_needed([(kv[by], side_starts(core, y, start_of, by)) for by in (1, 3)], True, nearest)


def attend(docs, qs, kv, states, chunk, head_dim, scale):
    smem = pl.BlockSpec(memory_space=pltpu.SMEM)
    vmem = pl.BlockSpec(memory_space=pltpu.VMEM)
    rows = qs[0].shape[0] * (qs[0].shape[1] // head_dim)
    names, arrays = tuple(kv), list(kv.values())
    keys = sum(array.shape[0] for array in arrays)
    given = list(states or [])
    out = [jax.ShapeDtypeStruct((head_dim + 8, rows), jnp.float32)] * len(qs)
    if states is None:
        out += [jax.ShapeDtypeStruct((1, qs[0].shape[0]), jnp.int32)]
    return pl.pallas_call(
        functools.partial(attend_kernel, names, len(qs), chunk, scale, states is None),
        out_shape=out,
        in_specs=[smem if states is None else vmem] + [vmem] * (len(qs) + len(arrays) + len(given)),
        out_specs=[vmem] * len(out),
        compiler_params=pltpu.CompilerParams(vmem_limit_bytes=32 * 1024 * 1024),
        cost_estimate=pl.CostEstimate(
            flops=4 * keys * rows * len(qs) * head_dim,
            bytes_accessed=4 * rows * head_dim,
            transcendentals=keys * rows * len(qs),
        ),
    )(docs, *qs, *arrays, *given)


def merge_kernel(head_dim, scale, keep_ref, came_ref, out_ref):
    rows = out_ref.shape[0]
    for h in range(out_ref.shape[1] // head_dim):
        cols = slice(h * rows, (h + 1) * rows)
        m_a, m_b = keep_ref[head_dim : head_dim + 1, cols], came_ref[head_dim : head_dim + 1, cols]
        l_a, l_b = keep_ref[head_dim + 1 : head_dim + 2, cols], came_ref[head_dim + 1 : head_dim + 2, cols]
        top = jnp.maximum(m_a, m_b)
        w_a, w_b = jnp.exp2((m_a - top) * scale), jnp.exp2((m_b - top) * scale)
        total = l_a * w_a + l_b * w_b
        w_a, w_b = w_a / total, w_b / total
        result = keep_ref[:head_dim, cols] * w_a + came_ref[:head_dim, cols] * w_b
        out_ref[:, h * head_dim : (h + 1) * head_dim] = result.T.astype(out_ref.dtype)


def merge(keep, came, rows, head_dim, scale):
    vmem = pl.BlockSpec(memory_space=pltpu.VMEM)
    heads = keep.shape[1] // rows
    return pl.pallas_call(
        functools.partial(merge_kernel, head_dim, scale),
        out_shape=jax.ShapeDtypeStruct((rows, heads * head_dim), jnp.bfloat16),
        in_specs=[vmem, vmem],
        out_specs=vmem,
        compiler_params=pltpu.CompilerParams(vmem_limit_bytes=8 * 1024 * 1024),
    )(keep, came)


def on_device(queries, key_rows, value_rows, doc_lengths):
    row_count = queries.shape[0]
    chunk, head_dim = key_rows.shape
    scale = math.log2(math.e) / math.sqrt(head_dim)
    ctx = lax.axis_index("ctx")
    core = lax.axis_index("head") % NC

    own = jnp.concatenate([key_rows, value_rows], axis=1)
    own = lax.optimization_barrier(own)
    back8 = send(own, later_plane(2))
    back4 = send(own, later_plane(1))
    back8, back4, late_q = lax.optimization_barrier((back8, back4, queries))
    other_q = send(late_q, other_core)

    def round_x(by):
        return (ctx // 2) % NX + by >= NX

    def first(by):
        wraps = (core == X_FIRST) & round_x(by)
        parts = [jnp.where(wraps, back4, own), jnp.where(wraps, back8, back4), back8]
        return send(jnp.concatenate(parts, axis=0), first_axis(by))

    got = {by: first(by) for by in (2, 1, 3)}
    planes = [own, back4, back8]
    held = []
    for i, plane in enumerate(planes):
        held += [plane] + [got[by][i * chunk : (i + 1) * chunk] for by in (1, 2, 3)]
    held = jnp.concatenate(held + [own], axis=0)

    def second(by, chunks):
        begin = jnp.where(core == X_FIRST, ctx % 2 if by != 2 else 0, jnp.where(round_x(by), NY, 0))
        return send(lax.dynamic_slice_in_dim(held, begin * chunk, chunks * chunk, 0), second_axis(by))

    sides = {1: second(1, WIDE), 2: second(2, WIDE + 1), 3: second(3, WIDE)}
    last = {by: sides[by] for by in (1, 3)}
    call = functools.partial(attend, chunk=chunk, head_dim=head_dim, scale=scale)
    both = [queries, other_q]
    *states, docs = call(doc_lengths, both, {"own": held}, None)
    keep, away = call(docs, both, {2: sides[2]}, states)
    (away,) = call(docs, [other_q], last, [away])
    came = send(away, other_core)
    (keep,) = call(docs, [queries], last, [keep])
    return merge(keep, came, row_count, head_dim, scale)


def solution(mesh):
    return jax.shard_map(
        on_device,
        mesh=mesh,
        in_specs=(P("ctx", "head"), P(("ctx", "head"), None), P(("ctx", "head"), None), P()),
        out_specs=P("ctx", "head"),
        check_vma=False,
    )
```

```python
import functools
import math

import jax
import jax.numpy as jnp
from jax import lax
from jax.experimental import pallas as pl
from jax.experimental.pallas import tpu as pltpu
from jax.sharding import PartitionSpec as P

NEG = -1e30
FAR = -(1 << 20)

NZ, NX, NY, NC = 8, 4, 4, 2
PAIRS = NZ * NX

WIDE = 8
LAST = 8
NEAR = 4

X_FIRST = 1


def device_index(pair, y, core):
    z, x = divmod(pair, NX)
    y = y % NY
    return (z * NX * 2 + x * 2 + y % 2) * 4 + (y // 2) * NC + core


def send(array, move):
    pairs = []
    for pair in range(PAIRS):
        for y in range(NY):
            for core in range(NC):
                target = move(pair, y, core)
                if target is not None:
                    pairs.append((device_index(pair, y, core), device_index(*target)))
    return lax.ppermute(array, ("ctx", "head"), sorted(pairs))


def later_plane(by):
    return lambda pair, y, core: ((pair + by * NX) % PAIRS, y, core)


def along_x(pair, by):
    return pair - pair % NX + (pair + by) % NX


def first_axis(by):
    return lambda pair, y, core: (along_x(pair, by), y, core) if core == X_FIRST else (pair, y + by, core)


def second_axis(by):
    return lambda pair, y, core: (pair, y + by, core) if core == X_FIRST else (along_x(pair, by), y, core)


def other_core(pair, y, core):
    return (pair, y, 1 - core)


def place(row_count, chunk):
    ctx = lax.axis_index("ctx")
    head = lax.axis_index("head")
    core, y_hi = head % NC, head // NC
    pair, y = ctx // 2, y_hi * 2 + ctx % 2

    def start_of(back, turn):
        there = (y - turn + NY) % NY
        return (2 * (pair - back) + there % 2) * row_count + (there // 2) * (NC * chunk) + core * chunk

    return ctx, core, y, start_of


def near_starts(core, start_of):
    return [jnp.where(core == X_FIRST, start_of(i, 0), start_of(i // NY * NX, i % NY)) for i in range(WIDE)]


def far_starts(core, start_of):
    return [start_of(LAST, 0)] + [jnp.where(core == X_FIRST, FAR, start_of(LAST, turn)) for turn in (1, 2, 3)]


def side_starts(core, y, start_of, by):
    skip = (y + by) % 2 if by != 2 else 0
    return [
        jnp.where(core == X_FIRST, start_of(i + skip, by), start_of(i // NY * NX + by, i % NY)) for i in range(WIDE)
    ]


def attend_kernel(names, groups, chunk, scale, opening, *refs):
    docs = refs[0]
    q_refs = refs[1 : 1 + groups]
    kv = dict(zip(names, refs[1 + groups :]))
    refs = refs[1 + groups + len(names) :]
    rows = q_refs[0].shape[0]
    head_dim = kv[names[0]].shape[1] // 2
    heads_here = q_refs[0].shape[1] // head_dim
    row_m, row_l = slice(head_dim, head_dim + 1), slice(head_dim + 1, head_dim + 2)
    state = refs[:groups] if opening else refs[groups:]
    for group, ref in enumerate(state):
        if opening:
            ref[...] = jnp.zeros(ref.shape, jnp.float32)
            ref[row_m, :] = jnp.full((1, ref.shape[1]), NEG, jnp.float32)
        else:
            ref[...] = refs[group][...]

    ctx, core, y, start_of = place(rows, chunk)
    first_row = ctx * rows
    last_row = first_row + (rows - 1)
    q_pos = first_row + lax.broadcasted_iota(jnp.int32, (1, rows), 1)
    if opening:
        end = jnp.int32(0)
        doc_start = jnp.zeros((1, rows), jnp.int32)
        for i in range(docs.shape[0]):
            end = end + docs[i]
            doc_start = jnp.where(end <= q_pos, end, doc_start)
        refs[groups][...] = doc_start
    else:
        doc_start = docs[...]
    first_doc, last_doc = jnp.min(doc_start), jnp.max(doc_start)

    def absorb(tiles, masked):
        keys_of, values_of, allowed = [], [], []
        for tile, starts in tiles:
            keys_of.append(tile[:, :head_dim])
            ones = jnp.ones((16, tile.shape[0]), tile.dtype)
            values_of.append(jnp.concatenate([tile[:, head_dim:].T, ones], axis=0))
            if masked:
                step = lax.broadcasted_iota(jnp.int32, (chunk, 1), 0)
                past = jnp.concatenate([step + start for start in starts], axis=0) - doc_start
                allowed.append(past.astype(jnp.uint32) <= (q_pos - doc_start).astype(jnp.uint32))

        def scores(t, group, h):
            return lax.dot_general(
                keys_of[t],
                q_refs[group][:, h * head_dim : (h + 1) * head_dim],
                (((1,), (1,)), ((), ())),
                preferred_element_type=jnp.float32,
            )

        def finish(t, group, h, p, alpha):
            ref, cols = state[group], slice(h * rows, (h + 1) * rows)
            out = jnp.dot(values_of[t], p, preferred_element_type=jnp.float32)
            ref[row_l, cols] = ref[row_l, cols] * alpha + out[head_dim : head_dim + 1]
            ref[:head_dim, cols] = ref[:head_dim, cols] * alpha + out[:head_dim]

        units = [(t, group, h) for t in range(len(tiles)) for group in range(groups) for h in range(heads_here)]
        ahead = [scores(*units[0]), scores(*units[1])]
        waiting = None
        for j, (t, group, h) in enumerate(units):
            ref, cols = state[group], slice(h * rows, (h + 1) * rows)
            s = ahead.pop(0)
            if j + 2 < len(units):
                ahead.append(scores(*units[j + 2]))
            if masked:
                s = jnp.where(allowed[t], s, NEG)
            m_old = ref[row_m, cols]
            m_new = jnp.maximum(m_old, jnp.max(s, axis=0, keepdims=True))
            alpha = jnp.exp2((m_old - m_new) * scale)
            p = jnp.exp2((s - m_new) * scale).astype(jnp.bfloat16)
            ref[row_m, cols] = m_new
            if waiting is not None:
                finish(*waiting)
            waiting = (t, group, h, p, alpha)
        finish(*waiting)

    def reach_of(starts):
        needed, full = [], []
        for start in starts:
            needed.append((start + (chunk - 1) >= first_doc) & (start <= last_row))
            full.append((start >= last_doc) & (start + (chunk - 1) <= first_row))
        return functools.reduce(jnp.logical_or, needed), functools.reduce(jnp.logical_and, full)

    def absorb_needed(parts, may_be_full, choose=None):
        needed, full = reach_of([start for _, starts in parts for start in starts])
        beyond, _ = reach_of([start for _, starts in parts for start in starts[NEAR:]])

        def tiles(count):
            return [(ref[: len(starts[:count]) * chunk, :], starts[:count]) for ref, starts in parts]

        if choose is not None:
            picked, places, rest = choose(parts)
            more, _ = reach_of(rest)

            @pl.when(needed & jnp.logical_not(more))
            def _():
                absorb([(picked(), places)], True)

            needed = more

        @pl.when(needed & jnp.logical_not(beyond))
        def _():
            near = tiles(NEAR)
            absorb([(jnp.concatenate([t for t, _ in near], axis=0), [s for _, starts in near for s in starts])], True)

        if may_be_full:

            @pl.when(full)
            def _():
                absorb(tiles(None), False)

            beyond = beyond & jnp.logical_not(full)

        @pl.when(beyond)
        def _():
            absorb(tiles(None), True)

    def nearest(parts):
        (ref, starts), (back_ref, back_starts) = parts
        pick = [jnp.where(core == X_FIRST, a, b) for a, b in zip(back_starts[:2], starts[2:4])]
        left = [jnp.where(core == X_FIRST, b, a) for a, b in zip(back_starts[:2], starts[2:4])]

        def tile():
            other = jnp.where(core == X_FIRST, back_ref[: 2 * chunk, :], ref[2 * chunk : 4 * chunk, :])
            return jnp.concatenate([ref[: 2 * chunk, :], other], axis=0)

        return tile, starts[:2] + pick, starts[4:] + back_starts[2:] + left

    if "own" in kv:
        absorb_needed([(kv["own"], near_starts(core, start_of) + far_starts(core, start_of))], False)
    if 2 in kv:
        last = jnp.where(core == X_FIRST, start_of(LAST, 2), FAR)
        absorb_needed([(kv[2], side_starts(core, y, start_of, 2) + [last])], False)
    if 1 in kv:
        absorb_needed([(kv[by], side_starts(core, y, start_of, by)) for by in (1, 3)], True, nearest)


def attend(docs, qs, kv, states, chunk, head_dim, scale):
    smem = pl.BlockSpec(memory_space=pltpu.SMEM)
    vmem = pl.BlockSpec(memory_space=pltpu.VMEM)
    rows = qs[0].shape[0] * (qs[0].shape[1] // head_dim)
    names, arrays = tuple(kv), list(kv.values())
    keys = sum(array.shape[0] for array in arrays)
    given = list(states or [])
    out = [jax.ShapeDtypeStruct((head_dim + 8, rows), jnp.float32)] * len(qs)
    if states is None:
        out += [jax.ShapeDtypeStruct((1, qs[0].shape[0]), jnp.int32)]
    return pl.pallas_call(
        functools.partial(attend_kernel, names, len(qs), chunk, scale, states is None),
        out_shape=out,
        in_specs=[smem if states is None else vmem] + [vmem] * (len(qs) + len(arrays) + len(given)),
        out_specs=[vmem] * len(out),
        compiler_params=pltpu.CompilerParams(vmem_limit_bytes=32 * 1024 * 1024),
        cost_estimate=pl.CostEstimate(
            flops=4 * keys * rows * len(qs) * head_dim,
            bytes_accessed=4 * rows * head_dim,
            transcendentals=keys * rows * len(qs),
        ),
    )(docs, *qs, *arrays, *given)


def merge_kernel(head_dim, scale, keep_ref, came_ref, out_ref):
    rows = out_ref.shape[0]
    for h in range(out_ref.shape[1] // head_dim):
        cols = slice(h * rows, (h + 1) * rows)
        m_a, m_b = keep_ref[head_dim : head_dim + 1, cols], came_ref[head_dim : head_dim + 1, cols]
        l_a, l_b = keep_ref[head_dim + 1 : head_dim + 2, cols], came_ref[head_dim + 1 : head_dim + 2, cols]
        top = jnp.maximum(m_a, m_b)
        w_a, w_b = jnp.exp2((m_a - top) * scale), jnp.exp2((m_b - top) * scale)
        total = l_a * w_a + l_b * w_b
        w_a, w_b = w_a / total, w_b / total
        result = keep_ref[:head_dim, cols] * w_a + came_ref[:head_dim, cols] * w_b
        out_ref[:, h * head_dim : (h + 1) * head_dim] = result.T.astype(out_ref.dtype)


def merge(keep, came, rows, head_dim, scale):
    vmem = pl.BlockSpec(memory_space=pltpu.VMEM)
    heads = keep.shape[1] // rows
    return pl.pallas_call(
        functools.partial(merge_kernel, head_dim, scale),
        out_shape=jax.ShapeDtypeStruct((rows, heads * head_dim), jnp.bfloat16),
        in_specs=[vmem, vmem],
        out_specs=vmem,
        compiler_params=pltpu.CompilerParams(vmem_limit_bytes=8 * 1024 * 1024),
    )(keep, came)


def on_device(queries, key_rows, value_rows, doc_lengths):
    row_count = queries.shape[0]
    chunk, head_dim = key_rows.shape
    scale = math.log2(math.e) / math.sqrt(head_dim)
    ctx = lax.axis_index("ctx")
    core = lax.axis_index("head") % NC

    own = jnp.concatenate([key_rows, value_rows], axis=1)
    own = lax.optimization_barrier(own)
    back8 = send(own, later_plane(2))
    back4 = send(own, later_plane(1))
    back8, back4, late_q = lax.optimization_barrier((back8, back4, queries))
    other_q = send(late_q, other_core)

    def round_x(by):
        return (ctx // 2) % NX + by >= NX

    def first(by):
        wraps = (core == X_FIRST) & round_x(by)
        parts = [jnp.where(wraps, back4, own), jnp.where(wraps, back8, back4), back8]
        return send(jnp.concatenate(parts, axis=0), first_axis(by))

    got = {by: first(by) for by in (2, 1, 3)}
    planes = [own, back4, back8]
    held = []
    for i, plane in enumerate(planes):
        held += [plane] + [got[by][i * chunk : (i + 1) * chunk] for by in (1, 2, 3)]
    held = jnp.concatenate(held + [own], axis=0)

    def second(by, chunks):
        begin = jnp.where(core == X_FIRST, ctx % 2 if by != 2 else 0, jnp.where(round_x(by), NY, 0))
        return send(lax.dynamic_slice_in_dim(held, begin * chunk, chunks * chunk, 0), second_axis(by))

    sides = {1: second(1, WIDE), 3: second(3, WIDE), 2: second(2, WIDE + 1)}
    last = {by: sides[by] for by in (1, 3)}
    call = functools.partial(attend, chunk=chunk, head_dim=head_dim, scale=scale)
    both = [queries, other_q]
    *states, docs = call(doc_lengths, both, {"own": held}, None)
    keep, away = call(docs, both, {2: sides[2]}, states)
    (away,) = call(docs, [other_q], last, [away])
    came = send(away, other_core)
    (keep,) = call(docs, [queries], last, [keep])
    return merge(keep, came, row_count, head_dim, scale)


def solution(mesh):
    return jax.shard_map(
        on_device,
        mesh=mesh,
        in_specs=(P("ctx", "head"), P(("ctx", "head"), None), P(("ctx", "head"), None), P()),
        out_specs=P("ctx", "head"),
        check_vma=False,
    )
```
